256 devices in a mesh: seq: 32 (over z, x), head: 8 (over y, core).
Axes of the slice: x: 4, y: 4, z: 8, core: 2. Of those that a mesh axis runs over, the one named last changes fastest.
Arguments:
- points: bfloat16 [65536, 512], P('seq'), may hold values from -12 to 12
- latents: bfloat16 [2048, 1536], replicated, may hold values from -12 to 12
- gain_in: float32 [512], replicated, may hold values from 0.1 to 1.9
- gain_lat: float32 [1536], replicated, may hold values from 0.1 to 1.9
- gain_self: float32 [1536], replicated, may hold values from 0.1 to 1.9
- cross_query: bfloat16 [1536, 1536], P(None, 'head'), may hold values from -1 to 1
- cross_key: bfloat16 [512, 1536], P(None, 'head'), may hold values from -1 to 1
- cross_value: bfloat16 [512, 1536], P(None, 'head'), may hold values from -0.25 to 0.25
- cross_out: bfloat16 [1536, 1536], P('head'), may hold values from -0.15625 to 0.15625
- self_query: bfloat16 [1536, 1536], P(None, 'head'), may hold values from -1 to 1
- latent_key_weight: bfloat16 [1536, 1536], P(None, 'head'), may hold values from -1 to 1
- self_value: bfloat16 [1536, 1536], P(None, 'head'), may hold values from -0.15625 to 0.15625
- self_out: bfloat16 [1536, 1536], P('head'), may hold values from -0.15625 to 0.15625
Outputs:
- encoded: bfloat16 [2048, 1536], P('seq', 'head')
The draws below stay inside these ranges and needn't reach their ends.
All inputs are finite; a program needn't handle non-finite values.
Results may differ from the reference program's by a relative error of at most 0.012.
Values may be sent and summed in bfloat16 or wider, within the bound.
No kernel may reach another device: no remote copies, remote signals or barrier semaphores. Data moves between devices by JAX's collectives and lax.ppermute only.
A program may use at most 128 MiB of HBM per device.

```python
import jax
import jax.numpy as jnp
from jax import lax

C = 512
D = 1536
HEADS = 16
N_LAT = 2048
HS = 96
POINTS = 65536


def shared_signs(key, length, salt):
    picks = jax.random.randint(jax.random.fold_in(key, salt), (length,), 0, 2)
    return picks.astype(jnp.float32) * 2.0 - 1.0


def projection(key, rows, cols, factor, left, right, weight):
    base = jnp.clip(jax.random.normal(key, (rows, cols), jnp.float32), -6.0, 6.0) * (factor / rows ** 0.5)
    return jnp.clip(base + weight * left[:, None] * right[None, :] / rows, -1.0, 1.0)


def draw_latents(key, part):
    key = jax.random.fold_in(key, 1)
    return jnp.clip(jax.random.normal(key, (N_LAT, D), jnp.float32), -6.0, 6.0).astype(jnp.bfloat16)


def draw_points(key, part):
    key = jax.random.fold_in(key, 2)
    return jnp.clip(jax.random.normal(key, (POINTS, C), jnp.float32), -6.0, 6.0).astype(jnp.bfloat16)


def draw_cross_query(key, part):
    left = shared_signs(key, D, 101)
    right = shared_signs(key, D, 103)
    key = jax.random.fold_in(key, 3)
    return projection(key, D, D, 3.0, left, right, 0.0).astype(jnp.bfloat16)


def draw_cross_key(key, part):
    left = shared_signs(key, C, 102)
    right = shared_signs(key, D, 103)
    key = jax.random.fold_in(key, 4)
    return projection(key, C, D, 1.0, left, right, 0.0).astype(jnp.bfloat16)


def draw_self_query(key, part):
    left = shared_signs(key, D, 101)
    right = shared_signs(key, D, 103)
    key = jax.random.fold_in(key, 5)
    return projection(key, D, D, 2.0, left, right, 0.0).astype(jnp.bfloat16)


def draw_latent_key_weight(key, part):
    left = shared_signs(key, D, 101)
    right = shared_signs(key, D, 103)
    key = jax.random.fold_in(key, 6)
    return projection(key, D, D, 1.0, left, right, 0.0).astype(jnp.bfloat16)


def steps_of(stream_key, shape, cuts, low, high):
    def one(dim, shards_of):
        heights = jax.random.uniform(jax.random.fold_in(jax.random.fold_in(stream_key, 6), dim), (shards_of,), jnp.float32, low / len(cuts), high / len(cuts))
        return jnp.repeat(jnp.exp(heights), shape[dim] // shards_of).reshape((-1,) + (1,) * (len(shape) - dim - 1))

    factor_of = one(*cuts[0])
    for cut in cuts[1:]:
        factor_of = factor_of * one(*cut)
    return factor_of


def scatter_about(own_key, shape, scale, reach, cuts=(), dtype=jnp.bfloat16):
    values = jax.random.normal(own_key, shape, jnp.float32) * scale
    if len(cuts) > 0:
        values = steps_of(own_key, shape, cuts, -0.22, 0.18) * values
    return jnp.clip(values, min=-reach, max=reach).astype(dtype)


def setup_inputs(seed: int = 0) -> dict:
    key_of = jax.random.split(jax.random.key(seed), 14)
    return {
        "points": draw_points(jax.random.fold_in(key_of[13], 71), 0),
        "latents": draw_latents(jax.random.fold_in(key_of[13], 71), 0),
        "gain_in": jnp.clip(1.0 + 0.18 * jax.random.normal(key_of[2], (C,), jnp.float32), 0.1, 1.9),
        "gain_lat": jnp.clip(1.0 + 0.18 * jax.random.normal(key_of[3], (D,), jnp.float32), 0.1, 1.9),
        "gain_self": jnp.clip(1.0 + 0.18 * jax.random.normal(key_of[4], (D,), jnp.float32), 0.1, 1.9),
        "cross_query": draw_cross_query(jax.random.fold_in(key_of[13], 71), 0),
        "cross_key": draw_cross_key(jax.random.fold_in(key_of[13], 71), 0),
        "cross_value": scatter_about(key_of[7], (C, D), C ** -0.5, 0.25, ((1, 8),)),
        "cross_out": scatter_about(key_of[8], (D, D), D ** -0.5, 0.15625, ((0, 8),)),
        "self_query": draw_self_query(jax.random.fold_in(key_of[13], 71), 0),
        "latent_key_weight": draw_latent_key_weight(jax.random.fold_in(key_of[13], 71), 0),
        "self_value": scatter_about(key_of[11], (D, D), D ** -0.5, 0.15625, ((1, 8),)),
        "self_out": scatter_about(key_of[12], (D, D), D ** -0.5, 0.15625, ((0, 8),)),
    }


def layer_norm(values, gain):
    values = values.astype(jnp.float32)
    center = values - lax.optimization_barrier(jnp.mean(values, axis=-1, keepdims=True))
    spread = lax.optimization_barrier(jnp.mean(center * center, axis=-1, keepdims=True))
    return center * lax.rsqrt(spread + 1e-05) * gain

def attend_head(inputs):
    query_h, keys_h, values_h = inputs
    block = min(256, N_LAT)
    blocks = query_h.reshape(N_LAT // block, block, HS)

    def one_block(query_b):
        scores = jnp.dot(query_b, keys_h.T, preferred_element_type=jnp.float32) * HS ** (-0.5)
        top = lax.optimization_barrier(jnp.max(scores, axis=1, keepdims=True))
        weights = jnp.exp(scores - top)
        total = lax.optimization_barrier(jnp.sum(weights, axis=1, keepdims=True))
        numer = jnp.dot(weights.astype(jnp.bfloat16), values_h, preferred_element_type=jnp.float32)
        return numer / total
    return lax.map(one_block, blocks).reshape(N_LAT, HS)

def split_heads(matrix):
    return matrix.reshape(matrix.shape[0], HEADS, HS).transpose(1, 0, 2)

def attend_block(query, keys, values):
    result = lax.map(attend_head, (split_heads(query), split_heads(keys), split_heads(values)))
    return result.transpose(1, 0, 2).reshape(N_LAT, D).astype(jnp.bfloat16)

def reference(points, latents, gain_in, gain_lat, gain_self, cross_query, cross_key, cross_value, cross_out, self_query, latent_key_weight, self_value, self_out):
    lat_normed = layer_norm(latents, gain_lat).astype(jnp.bfloat16)
    query = jnp.dot(lat_normed, cross_query, preferred_element_type=jnp.float32).astype(jnp.bfloat16)
    pts_normed = layer_norm(points, gain_in).astype(jnp.bfloat16)
    keys = jnp.dot(pts_normed, cross_key, preferred_element_type=jnp.float32).astype(jnp.bfloat16)
    values = jnp.dot(pts_normed, cross_value, preferred_element_type=jnp.float32).astype(jnp.bfloat16)
    cross_attn = attend_block(query, keys, values)
    middle = latents.astype(jnp.float32) + jnp.dot(cross_attn, cross_out, preferred_element_type=jnp.float32)
    latent_normalized = layer_norm(middle, gain_self).astype(jnp.bfloat16)
    latent_query_rows = jnp.dot(latent_normalized, self_query, preferred_element_type=jnp.float32).astype(jnp.bfloat16)
    latent_key_rows = jnp.dot(latent_normalized, latent_key_weight, preferred_element_type=jnp.float32).astype(jnp.bfloat16)
    latent_value_rows = jnp.dot(latent_normalized, self_value, preferred_element_type=jnp.float32).astype(jnp.bfloat16)
    latent_self_attention = attend_block(latent_query_rows, latent_key_rows, latent_value_rows)
    encoded = middle + jnp.dot(latent_self_attention, self_out, preferred_element_type=jnp.float32)
    return encoded.astype(jnp.bfloat16)
```

```python
import jax
import jax.numpy as jnp
from jax import lax
from jax.sharding import PartitionSpec as P

HS = 96
NX = 4
NY = 4
NZ = 8
X_GROUPS = [[z * NX + x for x in range(NX)] for z in range(NZ)]
Z_GROUPS = [[z * NX + x for z in range(NZ)] for x in range(NX)]
SHIFTS = (1, NX - 1, 2)


def layer_norm(values, gain):
    values = values.astype(jnp.float32)
    center = values - jnp.mean(values, axis=-1, keepdims=True)
    spread = jnp.mean(center * center, axis=-1, keepdims=True)
    return center * lax.rsqrt(spread + 1e-05) * gain


def project_rows(left, right):
    return jnp.dot(left, right, preferred_element_type=jnp.float32).astype(jnp.bfloat16)


def permute_x(v, k):
    return lax.ppermute(
        v, "seq", [(i, (i // NX) * NX + (i % NX + k) % NX) for i in range(NX * NZ)]
    )


def permute_y(v, k):
    return lax.ppermute(v, "head", [(i, (i + 2 * k) % (2 * NY)) for i in range(2 * NY)])


def swap_cores(v):
    return lax.ppermute(v, "head", [(i, i ^ 1) for i in range(2 * NY)])


def split_pair(value):
    high = lax.reduce_precision(value, 8, 7)
    low = lax.reduce_precision(value - high, 8, 7)
    return high, low


def pack(numer, total, shift):
    rows = numer.shape[:-2]
    parts = [numer.reshape(rows + (2 * HS,))]
    for value in (total, shift):
        parts.extend(split_pair(value))
    parts.append(jnp.zeros(rows + (256 - 2 * HS - 8,), jnp.float32))
    return jnp.concatenate(parts, axis=-1).astype(jnp.bfloat16)


def combine(packed):
    packed = packed.astype(jnp.float32)
    base = 2 * HS
    numer = packed[..., :base].reshape(packed.shape[:-1] + (2, HS))
    total = packed[..., base : base + 2] + packed[..., base + 2 : base + 4]
    shift = packed[..., base + 4 : base + 6] + packed[..., base + 6 : base + 8]
    high, low = split_pair(jnp.max(shift, axis=0))
    top = high + low
    scale = jnp.exp(shift - top)
    return jnp.sum(numer * scale[..., None], axis=0), jnp.sum(total * scale, axis=0), top


def attend(query, keys, values):
    scores = jnp.einsum("nhd,phd->hnp", query, keys, preferred_element_type=jnp.float32) * HS ** (-0.5)
    high, low = split_pair(jnp.max(scores, axis=2))
    top = high + low
    weights = jnp.exp(scores - top[:, :, None])
    total = jnp.sum(weights, axis=2)
    numer = jnp.einsum(
        "hnp,phd->nhd", weights.astype(jnp.bfloat16), values, preferred_element_type=jnp.float32
    )
    return numer, total.T, top.T


def body(
    points,
    latents,
    gain_in,
    gain_lat,
    gain_self,
    cross_query,
    cross_key,
    cross_value,
    cross_out,
    self_query,
    latent_key_weight,
    self_value,
    self_out,
):
    width = cross_query.shape[1]
    count, depth = latents.shape
    rows = count // (NX * NZ)
    seq = lax.axis_index("seq")
    head = lax.axis_index("head")

    near = [cross_out] + [permute_y(cross_out, k) for k in SHIFTS]
    near = jnp.concatenate(near, axis=0)
    out_all = jnp.concatenate([near, swap_cores(near)], axis=0)
    pair = 2 * width
    y = head // 2
    mine = [
        lax.dynamic_slice_in_dim(self_out, ((y + k) % NY) * pair, pair, 1) for k in (0,) + SHIFTS
    ]
    mine = [mine[0]] + [permute_y(v, k) for v, k in zip(mine[1:], SHIFTS)]
    mine = jnp.concatenate(mine, axis=0)
    core = head % 2
    own = lax.dynamic_slice_in_dim(mine, core * width, width, 1)
    other = swap_cores(lax.dynamic_slice_in_dim(mine, (1 - core) * width, width, 1))
    self_cols = jnp.concatenate([own, other], axis=0)

    def gather_heads(v):
        near = jnp.concatenate([v] + [permute_y(v, k) for k in SHIFTS], axis=1)
        return jnp.concatenate([near, swap_cores(near)], axis=1)

    lat_normed = layer_norm(latents, gain_lat).astype(jnp.bfloat16)
    query = project_rows(lat_normed, cross_query).reshape(count, 2, HS)
    pts_normed = layer_norm(points, gain_in).astype(jnp.bfloat16)
    keys = project_rows(pts_normed, cross_key).reshape(points.shape[0], 2, HS)
    values = project_rows(pts_normed, cross_value).reshape(points.shape[0], 2, HS)
    packed = pack(*attend(query, keys, values))
    packed = packed.reshape(NZ, NX, rows, 256).transpose(1, 0, 2, 3)
    packed = lax.all_to_all(packed, "seq", 0, 0, axis_index_groups=X_GROUPS)
    packed = pack(*combine(packed))
    packed = lax.all_to_all(packed, "seq", 0, 0, axis_index_groups=Z_GROUPS)
    numer, total, _ = combine(packed)
    cross_attn = (numer / total[:, :, None]).reshape(rows, width).astype(jnp.bfloat16)

    cross_term = jnp.dot(gather_heads(cross_attn), out_all, preferred_element_type=jnp.float32)
    lat_rows = lax.dynamic_slice_in_dim(latents, seq * rows, rows, 0)
    middle = lat_rows.astype(jnp.float32) + cross_term
    mid_normed = layer_norm(middle, gain_self).astype(jnp.bfloat16)
    squery = project_rows(mid_normed, self_query)
    skeys = project_rows(mid_normed, latent_key_weight)
    svalues = project_rows(mid_normed, self_value)

    key_values = jnp.concatenate([skeys, svalues], axis=1)
    key_values = jnp.broadcast_to(key_values[None], (NZ, rows, 2 * width))
    key_values = lax.all_to_all(key_values, "seq", 0, 0, axis_index_groups=Z_GROUPS)
    key_values = key_values.reshape(NZ * rows, 2 * width)
    squeries = jnp.concatenate([squery] + [permute_x(squery, k) for k in SHIFTS], axis=0)
    part = pack(
        *attend(
            squeries.reshape(NX * rows, 2, HS),
            key_values[:, :width].reshape(NZ * rows, 2, HS),
            key_values[:, width:].reshape(NZ * rows, 2, HS),
        )
    ).reshape(NX, rows, 256)
    back = [part[0]] + [permute_x(part[i + 1], -k) for i, k in enumerate(SHIFTS)]
    numer, total, _ = combine(jnp.stack(back))
    self_attn = (numer / total[:, :, None]).reshape(rows, width).astype(jnp.bfloat16)

    self_term = jnp.dot(gather_heads(self_attn), self_cols, preferred_element_type=jnp.float32)
    mid_cols = lax.dynamic_slice_in_dim(middle, head * width, width, 1)
    return (mid_cols + self_term).astype(jnp.bfloat16)


def solution(mesh):
    in_specs = (
        P("seq", None),
        P(),
        P(),
        P(),
        P(),
        P(None, "head"),
        P(None, "head"),
        P(None, "head"),
        P("head", None),
        P(None, "head"),
        P(None, "head"),
        P(None, "head"),
        P("head", None),
    )
    out_specs = P("seq", "head")
    return jax.shard_map(body, mesh=mesh, in_specs=in_specs, out_specs=out_specs, check_vma=False)
```

```python
import functools
import jax
import jax.numpy as jnp
from jax import lax
from jax.experimental import pallas as pl
from jax.experimental.pallas import tpu as pltpu
from jax.sharding import PartitionSpec as P

NX = 4
NY = 4
NZ = 8
Z_GROUPS = [[z * NX + x for z in range(NZ)] for x in range(NX)]
SHIFTS = (1, NX - 1, 2)

HS = 96
AUG = 112
LANES = 256
CHUNK = 256
LOG2E = 1.4426950408889634
SAFE = 64.0
F32 = jnp.float32
BF16 = jnp.bfloat16
NT = (((1,), (1,)), ((), ()))
VMEM_LIMIT = 48 * 1024 * 1024


def normed(values, gain):
    values = values.astype(F32)
    center = values - jnp.mean(values, axis=-1, keepdims=True)
    spread = jnp.mean(center * center, axis=-1, keepdims=True)
    return (center * lax.rsqrt(spread + 1e-05) * gain).astype(BF16)


def split_pair(value):
    high = value.astype(BF16).astype(F32)
    return high, (value - high).astype(BF16).astype(F32)


def key_value_kernel(points, gain, wk, wv, keys, values_t):
    step = 256
    wvt = wv[...].astype(F32).T.astype(BF16)
    for i in range(points.shape[0] // step):
        rows = pl.ds(i * step, step)
        x = normed(points[rows, :], gain[...])
        keys[rows, :] = jnp.dot(x, wk[...], preferred_element_type=F32).astype(BF16)
        vt = lax.dot_general(wvt, x, NT, preferred_element_type=F32).astype(BF16)
        for h in range(2):
            values_t[h, 0:HS, rows] = vt[h * HS : (h + 1) * HS]
    one = (lax.broadcasted_iota(jnp.int32, (AUG - HS, points.shape[0]), 0) == 0).astype(BF16)
    for h in range(2):
        values_t[h, HS:AUG, :] = one


def attend_units(queries, keys, values_t, sbuf, pbuf, emit):
    count = keys.shape[0]
    scale = LOG2E * HS ** (-0.5)

    def first(u):
        h, q = queries[u]
        s = lax.dot_general(keys[0:CHUNK, :], q, NT, preferred_element_type=F32)
        sbuf[u % 2] = s
        top = jnp.max(s, axis=0, keepdims=True)
        high, low = split_pair(top * scale)
        return top, high, low

    state = first(0)
    above = jnp.zeros((1, LANES), F32)
    for u, (h, q) in enumerate(queries):
        top, high, low = state
        shift = high + low
        for c in range(count // CHUNK):
            rows = pl.ds(c * CHUNK, CHUNK)
            if c == 0:
                s = sbuf[u % 2]
            else:
                s = lax.dot_general(
                    keys[rows, :], q, NT, preferred_element_type=F32
                )
                top = jnp.maximum(top, jnp.max(s, axis=0, keepdims=True))
            pbuf[u % 2, rows, :] = jnp.exp2(s * scale - shift).astype(BF16)
        if u + 1 < len(queries):
            state = first(u + 1)
        emit(u, jnp.dot(values_t[h], pbuf[u % 2], preferred_element_type=F32), high, low)
        above = jnp.maximum(above, top * scale - shift)
    return jnp.max(above)


def attend_exact(h, q, keys, values_t):
    scale = LOG2E * HS ** (-0.5)
    chunks = keys.shape[0] // CHUNK

    def scores(c):
        rows = pl.ds(pl.multiple_of(c * CHUNK, CHUNK), CHUNK)
        s = lax.dot_general(keys[rows, :], q, NT, preferred_element_type=F32)
        return s * scale

    def largest(c, top):
        return jnp.maximum(top, jnp.max(scores(c), axis=0, keepdims=True))

    top = lax.fori_loop(0, chunks, largest, jnp.full((1, LANES), -jnp.inf, F32))
    high, low = split_pair(top)
    shift = high + low

    def add(c, acc):
        rows = pl.ds(pl.multiple_of(c * CHUNK, CHUNK), CHUNK)
        p = jnp.exp2(scores(c) - shift).astype(BF16)
        return acc + jnp.dot(values_t[h, :, rows], p, preferred_element_type=F32)

    acc = lax.fori_loop(0, chunks, add, jnp.zeros((AUG, LANES), F32))
    return acc, high, low


def with_stats(acc, total, high, low):
    total_high, total_low = split_pair(total)
    row = lax.broadcasted_iota(jnp.int32, (AUG - HS, acc.shape[1]), 0)
    stats = jnp.where(row == 0, total_high, 0.0)
    stats = jnp.where(row == 1, total_low, stats)
    stats = jnp.where(row == 2, high, stats)
    stats = jnp.where(row == 3, low, stats)
    return jnp.concatenate([acc[:HS], stats], axis=0).astype(BF16)


def cross_kernel(where, latents, gain, wq, keys, values_t, out, qbuf, sbuf, pbuf, nbuf):
    del where
    nz, _, rows, _ = latents.shape
    for z in range(nz):
        x = normed(latents[z, 0], gain[...])
        qbuf[z * rows : (z + 1) * rows, :] = jnp.dot(
            x, wq[...], preferred_element_type=F32
        ).astype(BF16)
    blocks = nz * rows // LANES
    per = LANES // rows

    def query(j, h):
        start = j * LANES if isinstance(j, int) else pl.multiple_of(j * LANES, LANES)
        q = qbuf[pl.ds(start, LANES), :]
        lane = lax.broadcasted_iota(jnp.int32, q.shape, 1)
        return jnp.where((lane < HS) == (h == 0), q, jnp.zeros_like(q))

    def emit_at(j, h, acc, high, low):
        nbuf[h] = with_stats(acc, acc[HS : HS + 1], high, low)
        if h == 1:
            for i in range(per):
                lanes = slice(i * rows, (i + 1) * rows)
                out[j * per + i] = jnp.concatenate([nbuf[0, :, lanes], nbuf[1, :, lanes]], axis=1)

    queries = [(h, query(j, h)) for j in range(blocks) for h in range(2)]
    above = attend_units(
        queries, keys, values_t, sbuf, pbuf, lambda u, *r: emit_at(u // 2, u % 2, *r)
    )

    @pl.when(above > SAFE)
    def _():
        def again(j, carry):
            for h in range(2):
                emit_at(j, h, *attend_exact(h, query(j, h), keys, values_t))
            return carry

        lax.fori_loop(0, blocks, again, 0)


def whole():
    return pl.BlockSpec(memory_space=pltpu.VMEM)


def key_value_call(points, gain, wk, wv):
    n = points.shape[0]
    return pl.pallas_call(
        key_value_kernel,
        out_shape=(
            jax.ShapeDtypeStruct((n, 2 * HS), BF16),
            jax.ShapeDtypeStruct((2, AUG, n), BF16),
        ),
        in_specs=[whole()] * 4,
        out_specs=(whole(), whole()),
        compiler_params=pltpu.CompilerParams(vmem_limit_bytes=VMEM_LIMIT),
        cost_estimate=pl.CostEstimate(flops=16 * 10**8, bytes_accessed=4 * 10**6, transcendentals=0),
        name="key_value",
    )(points, gain, wk, wv)


def cross_call(where, latents, gain, wq, keys, values_t):
    nz, nx, rows, depth = latents.shape
    grid_spec = pltpu.PrefetchScalarGridSpec(
        num_scalar_prefetch=1,
        grid=(1,),
        in_specs=[
            pl.BlockSpec((nz, 1, rows, depth), lambda i, w: (0, w[0], 0, 0)),
            whole(), whole(), whole(), whole(),
        ],
        out_specs=whole(),
        scratch_shapes=[
            pltpu.VMEM((nz * rows, 2 * HS), BF16),
            pltpu.VMEM((2, CHUNK, LANES), F32),
            pltpu.VMEM((2, keys.shape[0], LANES), BF16),
            pltpu.VMEM((2, AUG, LANES), BF16),
        ],
    )
    return pl.pallas_call(
        cross_kernel,
        out_shape=jax.ShapeDtypeStruct((nz, AUG, 2 * rows), BF16),
        grid_spec=grid_spec,
        compiler_params=pltpu.CompilerParams(vmem_limit_bytes=VMEM_LIMIT),
        cost_estimate=pl.CostEstimate(
            flops=4 * 10**9, bytes_accessed=5 * 10**6, transcendentals=2 * 10**6
        ),
        name="cross",
    )(where, latents, gain, wq, keys, values_t)


def merge(parts):
    shifts = [p[HS + 2 : HS + 3] + p[HS + 3 : HS + 4] for p in parts]
    high, low = split_pair(functools.reduce(jnp.maximum, shifts))
    top = high + low
    acc = functools.reduce(jnp.add, [p * jnp.exp2(s - top) for p, s in zip(parts, shifts)])
    return acc, acc[HS : HS + 1] + acc[HS + 1 : HS + 2], high, low


def combine_kernel(a, b, c, d, out):
    for z in range(a.shape[0]):
        acc, total, high, low = merge([r[z].astype(F32) for r in (a, b, c, d)])
        out[z] = with_stats(acc, total, high, low)


def finish_kernel(*refs):
    out = refs[-1]
    parts = [r[i].astype(F32) for r in refs[:-1] for i in range(r.shape[0])]
    acc, total, _, _ = merge(parts)
    rows = out.shape[0]
    value = (acc[:HS] / total).T
    out[...] = jnp.concatenate([value[:rows], value[rows:]], axis=1).astype(BF16)


def middle_kernel(where, latents, gain, near, far, w0, w1, w2, w3, w4, w5, w6, w7, wq, wk, wv, mid, q, kv):
    del where
    rows, width = latents.shape[0], wq.shape[1]
    total = latents[...].astype(F32)
    for i, w in enumerate((w0, w1, w2, w3, w4, w5, w6, w7)):
        src = near if i < NY else far
        block = src[(i % NY) * rows : (i % NY + 1) * rows, :]
        total = total + jnp.dot(block, w[...], preferred_element_type=F32)
    mid[...] = total
    x = normed(total, gain[...])
    q[...] = jnp.dot(x, wq[...], preferred_element_type=F32).astype(BF16)
    kv[:, 0:width] = jnp.dot(x, wk[...], preferred_element_type=F32).astype(BF16)
    kv[:, width : 2 * width] = jnp.dot(x, wv[...], preferred_element_type=F32).astype(BF16)


def self_kernel(kv, q0, q1, q2, q3, out):
    scale = LOG2E * HS ** (-0.5)
    width = 2 * HS
    rows = q0.shape[0]
    keys = kv[:, 0:width]
    values_t = kv[:, width : 2 * width].astype(F32).T.astype(BF16)
    lane = lax.broadcasted_iota(jnp.int32, (rows, width), 1)
    first = lax.broadcasted_iota(jnp.int32, (HS, 2 * rows), 1) < rows
    for i, ref in enumerate((q0, q1, q2, q3)):
        q = ref[...]
        zero = jnp.zeros_like(q)
        both = jnp.concatenate([jnp.where(lane < HS, q, zero), jnp.where(lane < HS, zero, q)], axis=0)
        s = lax.dot_general(keys, both, NT, preferred_element_type=F32) * scale
        high, low = split_pair(jnp.max(s, axis=0, keepdims=True))
        p = jnp.exp2(s - (high + low))
        total = jnp.sum(p, axis=0, keepdims=True)
        n = jnp.dot(values_t, p.astype(BF16), preferred_element_type=F32)
        out[i] = with_stats(jnp.where(first, n[:HS], n[HS:]), total, high, low)


def output_kernel(mid, near, far, wn, wf, out):
    rows, width = out.shape
    total = jnp.zeros((rows, width), F32)
    for i in range(2 * NY):
        src, w = (near, wn) if i < NY else (far, wf)
        j = i % NY
        total = total + jnp.dot(
            src[j * rows : (j + 1) * rows, :],
            w[j * width : (j + 1) * width, :],
            preferred_element_type=F32,
        )
    out[...] = (mid[...] + total).astype(BF16)


def plain_call(kernel, name, out_shape, *args, flops=10**8):
    moved = sum(a.size * a.dtype.itemsize for a in args)
    return pl.pallas_call(
        kernel,
        out_shape=out_shape,
        in_specs=[whole()] * len(args),
        out_specs=jax.tree.map(lambda _: whole(), out_shape),
        compiler_params=pltpu.CompilerParams(vmem_limit_bytes=VMEM_LIMIT),
        cost_estimate=pl.CostEstimate(flops=flops, bytes_accessed=moved, transcendentals=0),
        name=name,
    )(*args)


def middle_call(where, latents, gain, near, far, weights, wq, wk, wv):
    rows, depth = near.shape[0] // NY, latents.shape[1]
    width = wq.shape[1]
    grid_spec = pltpu.PrefetchScalarGridSpec(
        num_scalar_prefetch=1,
        grid=(1,),
        in_specs=[pl.BlockSpec((rows, depth), lambda i, w: (w[0], 0))] + [whole()] * 14,
        out_specs=(whole(), whole(), whole()),
    )
    return pl.pallas_call(
        middle_kernel,
        out_shape=(
            jax.ShapeDtypeStruct((rows, depth), F32),
            jax.ShapeDtypeStruct((rows, width), BF16),
            jax.ShapeDtypeStruct((rows, 2 * width), BF16),
        ),
        grid_spec=grid_spec,
        compiler_params=pltpu.CompilerParams(vmem_limit_bytes=VMEM_LIMIT),
        cost_estimate=pl.CostEstimate(flops=4 * 10**8, bytes_accessed=7 * 10**6, transcendentals=0),
        name="middle",
    )(where, latents, gain, near, far, *weights, wq, wk, wv)


def permute_x(v, k):
    return lax.ppermute(
        v, "seq", [(i, (i // NX) * NX + (i % NX + k) % NX) for i in range(NX * NZ)]
    )


def permute_y(v, k):
    return lax.ppermute(v, "head", [(i, (i + 2 * k) % (2 * NY)) for i in range(2 * NY)])


def swap_cores(v):
    return lax.ppermute(v, "head", [(i, i ^ 1) for i in range(2 * NY)])


def gather_heads(v):
    near = jnp.concatenate([v] + [permute_y(v, k) for k in SHIFTS], axis=0)
    return near, swap_cores(near)


def body(
    points,
    latents,
    gain_in,
    gain_lat,
    gain_self,
    cross_query,
    cross_key,
    cross_value,
    cross_out,
    self_query,
    latent_key_weight,
    self_value,
    self_out,
):
    width = cross_query.shape[1]
    count, depth = latents.shape
    rows = count // (NX * NZ)
    seq = lax.axis_index("seq").astype(jnp.int32)
    head = lax.axis_index("head").astype(jnp.int32)
    part_shape = jax.ShapeDtypeStruct((NZ, AUG, 2 * rows), BF16)

    out_near = [cross_out] + [permute_y(cross_out, k) for k in SHIFTS]
    out_far = [swap_cores(v) for v in out_near]
    pair = 2 * width
    y, core = head // 2, head % 2
    mine = [
        lax.dynamic_slice_in_dim(self_out, ((y + k) % NY) * pair, pair, 1) for k in (0,) + SHIFTS
    ]
    mine = [mine[0]] + [permute_y(v, k) for v, k in zip(mine[1:], SHIFTS)]
    mine = jnp.concatenate(mine, axis=0)
    self_near = lax.dynamic_slice_in_dim(mine, core * width, width, 1)
    self_far = swap_cores(lax.dynamic_slice_in_dim(mine, (1 - core) * width, width, 1))

    keys, values_t = key_value_call(points, gain_in.reshape(1, -1), cross_key, cross_value)
    latents_4d = latents.reshape(NZ, NX, rows, depth)
    gain_row = gain_lat.reshape(1, -1)

    def chunk(k):
        x = ((seq % NX + k) % NX).reshape(1)
        return cross_call(x, latents_4d, gain_row, cross_query, keys, values_t)

    parts = [permute_x(chunk(k), k) for k in (2, 1, NX - 1)]
    part = plain_call(combine_kernel, "combine", part_shape, chunk(0), *parts)
    part = lax.all_to_all(part, "seq", 0, 0, axis_index_groups=Z_GROUPS)
    block = jax.ShapeDtypeStruct((rows, width), BF16)
    near, far = gather_heads(plain_call(finish_kernel, "finish", block, part))

    mid, squery, kv = middle_call(
        seq.reshape(1), latents, gain_self.reshape(1, -1), near, far, out_near + out_far,
        self_query, latent_key_weight, self_value,
    )
    kv = jnp.broadcast_to(kv[None], (NZ, rows, 2 * width))
    kv = lax.all_to_all(kv, "seq", 0, 0, axis_index_groups=Z_GROUPS)
    squeries = [squery] + [permute_x(squery, k) for k in SHIFTS]
    part = plain_call(
        self_kernel, "self_part", jax.ShapeDtypeStruct((NX, AUG, 2 * rows), BF16),
        kv.reshape(NZ * rows, 2 * width), *squeries,
    )
    back = [part[0:1]] + [permute_x(part[i + 1 : i + 2], -k) for i, k in enumerate(SHIFTS)]
    near, far = gather_heads(plain_call(finish_kernel, "finish_self", block, *back))
    mid_cols = lax.dynamic_slice_in_dim(mid, head * width, width, 1)
    return plain_call(output_kernel, "output", block, mid_cols, near, far, self_near, self_far)


def solution(mesh):
    in_specs = (
        P("seq", None),
        P(),
        P(),
        P(),
        P(),
        P(None, "head"),
        P(None, "head"),
        P(None, "head"),
        P("head", None),
        P(None, "head"),
        P(None, "head"),
        P(None, "head"),
        P("head", None),
    )
    out_specs = P("seq", "head")
    return jax.shard_map(body, mesh=mesh, in_specs=in_specs, out_specs=out_specs, check_vma=False)
```

```python
import functools
import jax
import jax.numpy as jnp
from jax import lax
from jax.experimental import pallas as pl
from jax.experimental.pallas import tpu as pltpu
from jax.sharding import PartitionSpec as P

NX = 4
NY = 4
NZ = 8
Z_GROUPS = [[z * NX + x for z in range(NZ)] for x in range(NX)]
SHIFTS = (1, NX - 1, 2)

HS = 96
AUG = 112
LANES = 256
CHUNK = 256
LOG2E = 1.4426950408889634
SAFE = 64.0
F32 = jnp.float32
BF16 = jnp.bfloat16
NT = (((1,), (1,)), ((), ()))
VMEM_LIMIT = 20 * 1024 * 1024


def normed(values, gain):
    values = values.astype(F32)
    center = values - jnp.mean(values, axis=-1, keepdims=True)
    spread = jnp.mean(center * center, axis=-1, keepdims=True)
    return (center * lax.rsqrt(spread + 1e-05) * gain).astype(BF16)


def gain_row(gain):
    return jnp.concatenate([gain[i : i + 1, :] for i in range(gain.shape[0])], axis=1)


def split_pair(value):
    high = value.astype(BF16).astype(F32)
    return high, (value - high).astype(BF16).astype(F32)


def key_value_kernel(points, gain, wk, wv, keys, values_t, xbuf):
    row = gain_row(gain)
    count, step = points.shape[0], 64
    for i in range(count // step):
        rows = pl.ds(i * step, step)
        xbuf[rows, :] = normed(points[rows, :], row)
    x = xbuf[...]
    keys[...] = lax.dot_general(x, wk[...], NT, preferred_element_type=F32).astype(BF16)
    vt = lax.dot_general(wv[...], x, NT, preferred_element_type=F32).astype(BF16)
    one = (lax.broadcasted_iota(jnp.int32, (AUG - HS, count), 0) == 0).astype(BF16)
    for h in range(2):
        values_t[h, 0:HS, :] = vt[h * HS : (h + 1) * HS]
        values_t[h, HS:AUG, :] = one


def attend_units(queries, keys, values_t, sbuf, pbuf, emit):
    count = keys.shape[0]
    scale = LOG2E * HS ** (-0.5)

    def first(u):
        h, q = queries[u]
        s = lax.dot_general(keys[0:CHUNK, :], q, NT, preferred_element_type=F32)
        sbuf[u % 2] = s
        top = jnp.max(s, axis=0, keepdims=True)
        high, low = split_pair(top * scale)
        return top, high, low

    state = first(0)
    above = jnp.zeros((1, LANES), F32)
    for u, (h, q) in enumerate(queries):
        top, high, low = state
        shift = high + low
        for c in range(count // CHUNK):
            rows = pl.ds(c * CHUNK, CHUNK)
            if c == 0:
                s = sbuf[u % 2]
            else:
                s = lax.dot_general(
                    keys[rows, :], q, NT, preferred_element_type=F32
                )
                top = jnp.maximum(top, jnp.max(s, axis=0, keepdims=True))
            pbuf[u % 2, rows, :] = jnp.exp2(s * scale - shift).astype(BF16)
        if u + 1 < len(queries):
            state = first(u + 1)
        emit(u, jnp.dot(values_t[h], pbuf[u % 2], preferred_element_type=F32), high, low)
        above = jnp.maximum(above, top * scale - shift)
    return jnp.max(above)


def attend_exact(h, q, keys, values_t):
    scale = LOG2E * HS ** (-0.5)
    chunks = keys.shape[0] // CHUNK

    def scores(c):
        rows = pl.ds(pl.multiple_of(c * CHUNK, CHUNK), CHUNK)
        s = lax.dot_general(keys[rows, :], q, NT, preferred_element_type=F32)
        return s * scale

    def largest(c, top):
        return jnp.maximum(top, jnp.max(scores(c), axis=0, keepdims=True))

    top = lax.fori_loop(0, chunks, largest, jnp.full((1, LANES), -jnp.inf, F32))
    high, low = split_pair(top)
    shift = high + low

    def add(c, acc):
        rows = pl.ds(pl.multiple_of(c * CHUNK, CHUNK), CHUNK)
        p = jnp.exp2(scores(c) - shift).astype(BF16)
        return acc + jnp.dot(values_t[h, :, rows], p, preferred_element_type=F32)

    acc = lax.fori_loop(0, chunks, add, jnp.zeros((AUG, LANES), F32))
    return acc, high, low


def with_stats(acc, total, high, low):
    total_high, total_low = split_pair(total)
    row = lax.broadcasted_iota(jnp.int32, (AUG - HS, acc.shape[1]), 0)
    stats = jnp.where(row == 0, total_high, 0.0)
    stats = jnp.where(row == 1, total_low, stats)
    stats = jnp.where(row == 2, high, stats)
    stats = jnp.where(row == 3, low, stats)
    return jnp.concatenate([acc[:HS], stats], axis=0).astype(BF16)


def cross_kernel(where, latents, gain, wq, keys, values_t, out, xbuf, qbuf, sbuf, pbuf, nbuf):
    nz, _, rows, _ = latents.shape
    row = gain_row(gain)
    for z in range(nz):
        xbuf[z * rows : (z + 1) * rows, :] = normed(latents[z, where[0]], row)
    qbuf[...] = lax.dot_general(xbuf[...], wq[...], NT, preferred_element_type=F32).astype(BF16)
    blocks = nz * rows // LANES
    per = LANES // rows

    def query(j, h):
        start = j * LANES if isinstance(j, int) else pl.multiple_of(j * LANES, LANES)
        q = qbuf[pl.ds(start, LANES), :]
        lane = lax.broadcasted_iota(jnp.int32, q.shape, 1)
        return jnp.where((lane < HS) == (h == 0), q, jnp.zeros_like(q))

    def emit_at(j, h, acc, high, low):
        nbuf[h] = with_stats(acc, acc[HS : HS + 1], high, low)
        if h == 1:
            for i in range(per):
                lanes = slice(i * rows, (i + 1) * rows)
                out[j * per + i] = jnp.concatenate([nbuf[0, :, lanes], nbuf[1, :, lanes]], axis=1)

    queries = [(h, query(j, h)) for j in range(blocks) for h in range(2)]
    above = attend_units(
        queries, keys, values_t, sbuf, pbuf, lambda u, *r: emit_at(u // 2, u % 2, *r)
    )

    @pl.when(above > SAFE)
    def _():
        def again(j, carry):
            for h in range(2):
                emit_at(j, h, *attend_exact(h, query(j, h), keys, values_t))
            return carry

        lax.fori_loop(0, blocks, again, 0)


def whole():
    return pl.BlockSpec(memory_space=pltpu.VMEM)


def key_value_call(points, gain, wk, wv):
    n, depth = points.shape
    step = n // 4
    return pl.pallas_call(
        key_value_kernel,
        out_shape=(
            jax.ShapeDtypeStruct((n, 2 * HS), BF16),
            jax.ShapeDtypeStruct((2, AUG, n), BF16),
        ),
        grid=(n // step,),
        in_specs=[pl.BlockSpec((step, depth), lambda i: (i, 0))] + [whole()] * 3,
        out_specs=(
            pl.BlockSpec((step, 2 * HS), lambda i: (i, 0)),
            pl.BlockSpec((2, AUG, step), lambda i: (0, 0, i)),
        ),
        scratch_shapes=[pltpu.VMEM((step, depth), BF16)],
        compiler_params=pltpu.CompilerParams(vmem_limit_bytes=VMEM_LIMIT),
        cost_estimate=pl.CostEstimate(flops=16 * 10**8, bytes_accessed=4 * 10**6, transcendentals=0),
        name="key_value",
    )(points, gain, wk, wv)


def cross_call(where, latents, gain, wq, keys, values_t):
    nz, nx, rows, depth = latents.shape
    return pl.pallas_call(
        cross_kernel,
        out_shape=jax.ShapeDtypeStruct((nz, AUG, 2 * rows), BF16),
        in_specs=[pl.BlockSpec(memory_space=pltpu.SMEM)] + [whole()] * 5,
        out_specs=whole(),
        scratch_shapes=[
            pltpu.VMEM((nz * rows, depth), BF16),
            pltpu.VMEM((nz * rows, 2 * HS), BF16),
            pltpu.VMEM((2, CHUNK, LANES), F32),
            pltpu.VMEM((2, keys.shape[0], LANES), BF16),
            pltpu.VMEM((2, AUG, LANES), BF16),
        ],
        compiler_params=pltpu.CompilerParams(vmem_limit_bytes=VMEM_LIMIT),
        cost_estimate=pl.CostEstimate(
            flops=4 * 10**9, bytes_accessed=5 * 10**6, transcendentals=2 * 10**6
        ),
        name="cross",
    )(where, latents, gain, wq, keys, values_t)


def merge(parts):
    shifts = [p[HS + 2 : HS + 3] + p[HS + 3 : HS + 4] for p in parts]
    high, low = split_pair(functools.reduce(jnp.maximum, shifts))
    top = high + low
    acc = functools.reduce(jnp.add, [p * jnp.exp2(s - top) for p, s in zip(parts, shifts)])
    return acc, acc[HS : HS + 1] + acc[HS + 1 : HS + 2], high, low


def combine_kernel(a, b, c, d, out):
    for z in range(a.shape[0]):
        acc, total, high, low = merge([r[z].astype(F32) for r in (a, b, c, d)])
        out[z] = with_stats(acc, total, high, low)


def finish_kernel(*refs):
    out = refs[-1]
    parts = [r[i].astype(F32) for r in refs[:-1] for i in range(r.shape[0])]
    acc, total, _, _ = merge(parts)
    rows = out.shape[0]
    value = (acc[:HS] / total).T
    out[...] = jnp.concatenate([value[:rows], value[rows:]], axis=1).astype(BF16)


def near_kernel(a0, a1, a2, a3, w0, w1, w2, w3, out):
    total = None
    for a, w in ((a0, w0), (a1, w1), (a2, w2), (a3, w3)):
        term = jnp.dot(a[...], w[...], preferred_element_type=F32)
        total = term if total is None else total + term
    out[...] = total


def middle_kernel(where, latents, gain, own, other, wq, wk, wv, mid, q, kv):
    rows, width = q.shape
    start = pl.multiple_of(where[0] * rows, rows)
    total = latents[pl.ds(start, rows), :].astype(F32) + (own[...] + other[...])
    mid[...] = total
    x = normed(total, gain_row(gain))
    q[...] = lax.dot_general(x, wq[...], NT, preferred_element_type=F32).astype(BF16)
    k = lax.dot_general(x, wk[...], NT, preferred_element_type=F32).astype(BF16)
    v = lax.dot_general(x, wv[...], NT, preferred_element_type=F32).astype(BF16)
    both = jnp.concatenate([k, v], axis=1)
    for i in range(kv.shape[0]):
        kv[i] = both


def self_kernel(kv, q0, q1, q2, q3, out):
    scale = LOG2E * HS ** (-0.5)
    width = 2 * HS
    rows = q0.shape[0]
    keys = kv[:, 0:width]
    values_t = kv[:, width : 2 * width].astype(F32).T.astype(BF16)
    lane = lax.broadcasted_iota(jnp.int32, (rows, width), 1)
    first = lax.broadcasted_iota(jnp.int32, (HS, 2 * rows), 1) < rows
    for i, ref in enumerate((q0, q1, q2, q3)):
        q = ref[...]
        zero = jnp.zeros_like(q)
        both = jnp.concatenate([jnp.where(lane < HS, q, zero), jnp.where(lane < HS, zero, q)], axis=0)
        s = lax.dot_general(keys, both, NT, preferred_element_type=F32) * scale
        high, low = split_pair(jnp.max(s, axis=0, keepdims=True))
        p = jnp.exp2(s - (high + low))
        total = jnp.sum(p, axis=0, keepdims=True)
        n = jnp.dot(values_t, p.astype(BF16), preferred_element_type=F32)
        out[i] = with_stats(jnp.where(first, n[:HS], n[HS:]), total, high, low)


def output_kernel(where, a0, a1, a2, a3, w, own, other):
    rows, width = a0.shape
    total = None
    for i, a in enumerate((a0, a1, a2, a3)):
        term = jnp.dot(a[...], w[i * width : (i + 1) * width, :], preferred_element_type=F32)
        total = term if total is None else total + term
    left, right = total[:, :width], total[:, width:]
    mine = where[0] == 0
    own[...] = jnp.where(mine, left, right)
    other[...] = jnp.where(mine, right, left)


def add_kernel(mid, own, other, out):
    out[...] = (mid[...] + (own[...] + other[...])).astype(BF16)


def plain_call(kernel, name, out_shape, *args, flops=10**8):
    moved = sum(a.size * a.dtype.itemsize for a in args)
    spec = lambda a: pl.BlockSpec(memory_space=pltpu.SMEM) if a.dtype == jnp.int32 else whole()
    return pl.pallas_call(
        kernel,
        out_shape=out_shape,
        in_specs=[spec(a) for a in args],
        out_specs=jax.tree.map(lambda _: whole(), out_shape),
        compiler_params=pltpu.CompilerParams(vmem_limit_bytes=VMEM_LIMIT),
        cost_estimate=pl.CostEstimate(flops=flops, bytes_accessed=moved, transcendentals=0),
        name=name,
    )(*args)


def permute_x(v, k):
    return lax.ppermute(
        v, "seq", [(i, (i // NX) * NX + (i % NX + k) % NX) for i in range(NX * NZ)]
    )


def permute_y(v, k):
    return lax.ppermute(v, "head", [(i, (i + 2 * k) % (2 * NY)) for i in range(2 * NY)])


def swap_cores(v):
    return lax.ppermute(v, "head", [(i, i ^ 1) for i in range(2 * NY)])


def gather_y(v):
    return [v] + [permute_y(v, k) for k in SHIFTS]


def body(
    points,
    latents,
    gain_in,
    gain_lat,
    gain_self,
    cross_query,
    cross_key,
    cross_value,
    cross_out,
    self_query,
    latent_key_weight,
    self_value,
    self_out,
):
    width = cross_query.shape[1]
    count, depth = latents.shape
    rows = count // (NX * NZ)
    seq = lax.axis_index("seq").astype(jnp.int32)
    head = lax.axis_index("head").astype(jnp.int32)
    part_shape = jax.ShapeDtypeStruct((NZ, AUG, 2 * rows), BF16)
    gains = [g.reshape(-1, 128) for g in (gain_in, gain_lat, gain_self)]

    keys, values_t = key_value_call(points, gains[0], cross_key.T, cross_value.T)
    keys, cross_out = lax.optimization_barrier((keys, cross_out))
    out_near = gather_y(cross_out)
    latents_4d = latents.reshape(NZ, NX, rows, depth)

    def chunk(k):
        x = ((seq % NX + k) % NX).reshape(1)
        return cross_call(x, latents_4d, gains[1], cross_query.T, keys, values_t)

    parts = [permute_x(chunk(k), k) for k in (2, 1, NX - 1)]
    part = plain_call(combine_kernel, "combine", part_shape, chunk(0), *parts)

    pair = 2 * width
    y, core = head // 2, head % 2
    part, self_out = lax.optimization_barrier((part, self_out))
    mine = [
        lax.dynamic_slice_in_dim(self_out, ((y + k) % NY) * pair, pair, 1) for k in (0,) + SHIFTS
    ]
    mine = [mine[0]] + [permute_y(v, k) for v, k in zip(mine[1:], SHIFTS)]
    mine = jnp.concatenate(mine, axis=0)

    part = lax.all_to_all(part, "seq", 0, 0, axis_index_groups=Z_GROUPS)
    part, mine, out_near = lax.optimization_barrier((part, mine, out_near))
    block = jax.ShapeDtypeStruct((rows, width), BF16)
    cross_attn = plain_call(finish_kernel, "finish", block, part)
    own = plain_call(
        near_kernel, "near", jax.ShapeDtypeStruct((rows, depth), F32), *gather_y(cross_attn), *out_near
    )
    mid, squery, kv = plain_call(
        middle_kernel, "middle",
        (
            jax.ShapeDtypeStruct((rows, depth), F32),
            block,
            jax.ShapeDtypeStruct((NZ, rows, pair), BF16),
        ),
        seq.reshape(1), latents, gains[2], own, swap_cores(own),
        self_query.T, latent_key_weight.T, self_value.T,
    )
    kv = lax.all_to_all(kv, "seq", 0, 0, axis_index_groups=Z_GROUPS)
    squeries = [squery] + [permute_x(squery, k) for k in SHIFTS]
    mid_cols = lax.dynamic_slice_in_dim(mid, head * width, width, 1)
    kv, mid_cols = lax.optimization_barrier((kv, mid_cols))
    part = plain_call(
        self_kernel, "self_part", jax.ShapeDtypeStruct((NX, AUG, 2 * rows), BF16),
        kv.reshape(NZ * rows, pair), *squeries,
    )
    back = [part[0:1]] + [permute_x(part[i + 1 : i + 2], -k) for i, k in enumerate(SHIFTS)]
    self_attn = plain_call(finish_kernel, "finish_self", block, *back)
    half = jax.ShapeDtypeStruct((rows, width), F32)
    own, give = plain_call(
        output_kernel, "output", (half, half), core.reshape(1), *gather_y(self_attn), mine
    )
    return plain_call(add_kernel, "add", block, mid_cols, own, swap_cores(give))


def solution(mesh):
    in_specs = (
        P("seq", None),
        P(),
        P(),
        P(),
        P(),
        P(None, "head"),
        P(None, "head"),
        P(None, "head"),
        P("head", None),
        P(None, "head"),
        P(None, "head"),
        P(None, "head"),
        P("head", None),
    )
    out_specs = P("seq", "head")
    return jax.shard_map(body, mesh=mesh, in_specs=in_specs, out_specs=out_specs, check_vma=False)
```

```python
import functools
import jax
import jax.numpy as jnp
from jax import lax
from jax.experimental import pallas as pl
from jax.experimental.pallas import tpu as pltpu
from jax.sharding import PartitionSpec as P

NX = 4
NY = 4
NZ = 8
Z_GROUPS = [[z * NX + x for z in range(NZ)] for x in range(NX)]
SHIFTS = (1, NX - 1, 2)
FOREIGN = (2, 1, NX - 1)

HS = 96
AUG = 112
LANES = 256
CHUNK = 256
PIECE = 512
SMALL = 16
LOG2E = 1.4426950408889634
SAFE = 64.0
F32 = jnp.float32
BF16 = jnp.bfloat16
NT = (((1,), (1,)), ((), ()))
VMEM_LIMIT = 20 * 1024 * 1024
VMEM_WIDE = 56 * 1024 * 1024


def normed(values, gain):
    values = values.astype(F32)
    center = values - jnp.mean(values, axis=-1, keepdims=True)
    spread = jnp.mean(center * center, axis=-1, keepdims=True)
    return (center * lax.rsqrt(spread + 1e-05) * gain).astype(BF16)


def gain_row(gain):
    return jnp.concatenate([gain[i : i + 1, :] for i in range(gain.shape[0])], axis=1)


def split_pair(value):
    high = value.astype(BF16).astype(F32)
    return high, (value - high).astype(BF16).astype(F32)


def fetch(pairs, sems):
    copies = [pltpu.make_async_copy(src, dst, sems.at[i]) for i, (src, dst) in enumerate(pairs)]
    for copy in copies:
        copy.start()
    return copies


def project_points(pbuf, row, wk, wv, keys, values_t, xbuf, ready):
    one = (lax.broadcasted_iota(jnp.int32, (AUG - HS, PIECE), 0) == 0).astype(BF16)
    for i in range(pbuf.shape[0] // PIECE):
        ready(i)
        rows = pl.ds(i * PIECE, PIECE)
        for j in range(0, PIECE, 64):
            xbuf[j : j + 64, :] = normed(pbuf[i * PIECE + j : i * PIECE + j + 64, :], row)
        x = xbuf[...]
        keys[rows, :] = lax.dot_general(x, wk[...], NT, preferred_element_type=F32).astype(BF16)
        vt = lax.dot_general(wv[...], x, NT, preferred_element_type=F32).astype(BF16)
        for h in range(2):
            values_t[h, 0:HS, rows] = vt[h * HS : (h + 1) * HS]
            values_t[h, HS:AUG, rows] = one


def attend_units(queries, keys, values_t, sbuf, pbuf, emit, between):
    count = keys.shape[0]
    scale = LOG2E * HS ** (-0.5)

    def first(u):
        h, q = queries[u]
        s = lax.dot_general(keys[0:CHUNK, :], q, NT, preferred_element_type=F32)
        sbuf[u % 2] = s
        top = jnp.max(s, axis=0, keepdims=True)
        high, low = split_pair(top * scale)
        return top, high, low

    state = first(0)
    above = jnp.zeros((1, LANES), F32)
    for u, (h, q) in enumerate(queries):
        top, high, low = state
        shift = high + low
        for c in range(count // CHUNK):
            rows = pl.ds(c * CHUNK, CHUNK)
            if c == 0:
                s = sbuf[u % 2]
            else:
                s = lax.dot_general(
                    keys[rows, :], q, NT, preferred_element_type=F32
                )
                top = jnp.maximum(top, jnp.max(s, axis=0, keepdims=True))
            pbuf[u % 2, rows, :] = jnp.exp2(s * scale - shift).astype(BF16)
            between()
        if u + 1 < len(queries):
            state = first(u + 1)
        emit(u, jnp.dot(values_t[h], pbuf[u % 2], preferred_element_type=F32), high, low)
        above = jnp.maximum(above, top * scale - shift)
    return jnp.max(above)


def attend_exact(h, q, keys, values_t):
    scale = LOG2E * HS ** (-0.5)
    chunks = keys.shape[0] // CHUNK

    def scores(c):
        rows = pl.ds(pl.multiple_of(c * CHUNK, CHUNK), CHUNK)
        s = lax.dot_general(keys[rows, :], q, NT, preferred_element_type=F32)
        return s * scale

    def largest(c, top):
        return jnp.maximum(top, jnp.max(scores(c), axis=0, keepdims=True))

    top = lax.fori_loop(0, chunks, largest, jnp.full((1, LANES), -jnp.inf, F32))
    high, low = split_pair(top)
    shift = high + low

    def add(c, acc):
        rows = pl.ds(pl.multiple_of(c * CHUNK, CHUNK), CHUNK)
        p = jnp.exp2(scores(c) - shift).astype(BF16)
        return acc + jnp.dot(values_t[h, :, rows], p, preferred_element_type=F32)

    acc = lax.fori_loop(0, chunks, add, jnp.zeros((AUG, LANES), F32))
    return acc, high, low


def with_stats(acc, total, high, low):
    total_high, total_low = split_pair(total)
    row = lax.broadcasted_iota(jnp.int32, (AUG - HS, acc.shape[1]), 0)
    stats = jnp.where(row == 0, total_high, 0.0)
    stats = jnp.where(row == 1, total_low, stats)
    stats = jnp.where(row == 2, high, stats)
    stats = jnp.where(row == 3, low, stats)
    return jnp.concatenate([acc[:HS], stats], axis=0).astype(BF16)


def attend_chunk(qbuf, keys, values_t, sbuf, pbuf, nbuf, out, between):
    rows = out.shape[2] // 2
    blocks = qbuf.shape[0] // LANES
    per = LANES // rows

    def query(j, h):
        start = j * LANES if isinstance(j, int) else pl.multiple_of(j * LANES, LANES)
        q = qbuf[pl.ds(start, LANES), :]
        lane = lax.broadcasted_iota(jnp.int32, q.shape, 1)
        return jnp.where((lane < HS) == (h == 0), q, jnp.zeros_like(q))

    def emit_at(j, h, acc, high, low):
        nbuf[h] = with_stats(acc, acc[HS : HS + 1], high, low)
        if h == 1:
            for i in range(per):
                lanes = slice(i * rows, (i + 1) * rows)
                out[j * per + i] = jnp.concatenate([nbuf[0, :, lanes], nbuf[1, :, lanes]], axis=1)

    queries = [(h, query(j, h)) for j in range(blocks) for h in range(2)]
    above = attend_units(
        queries, keys, values_t, sbuf, pbuf, lambda u, *r: emit_at(u // 2, u % 2, *r), between
    )

    @pl.when(above > SAFE)
    def _():
        def again(j, carry):
            for h in range(2):
                emit_at(j, h, *attend_exact(h, query(j, h), keys, values_t))
            return carry

        lax.fori_loop(0, blocks, again, 0)


def norm_pieces(lbuf, row, xbuf):
    rows = lbuf.shape[1]

    def piece(i):
        z, r = divmod(i * SMALL, rows)
        xbuf[i * SMALL : (i + 1) * SMALL, :] = normed(lbuf[z, r : r + SMALL, :], row)

    return [functools.partial(piece, i) for i in range(lbuf.shape[0] * rows // SMALL)]


def project_query(xbuf, wq, qbuf):
    qbuf[...] = lax.dot_general(xbuf[...], wq[...], NT, preferred_element_type=F32).astype(BF16)


def encode_kernel(
    where, points, latents, gain_in, gain_lat, wk_in, wv_in, wq_in,
    out0, out1, out2, keys_out, values_out,
    pts, lbuf, gbuf, hbuf, wk, wv, wq, keys, values_t, ybuf, xbuf, qbuf, sbuf, pbuf, nbuf, sems,
):
    outs = (out0, out1, out2)
    nz = lbuf.shape[1]
    pieces = pts.shape[0] // PIECE
    copies = fetch(
        [(gain_in, gbuf)]
        + [(points.at[pl.ds(i * PIECE, PIECE), :], pts.at[pl.ds(i * PIECE, PIECE), :]) for i in range(pieces)]
        + [(wk_in, wk), (wv_in, wv), (gain_lat, hbuf), (wq_in, wq)]
        + [(latents.at[:, lax.rem(where[0] + k, NX)], lbuf.at[i]) for i, k in enumerate(FOREIGN)],
        sems,
    )
    copies[0].wait()

    def ready(i):
        copies[1 + i].wait()
        if i == 0:
            copies[1 + pieces].wait()
            copies[2 + pieces].wait()

    project_points(pts, gain_row(gbuf), wk, wv, keys, values_t, ybuf, ready)
    back = fetch([(keys, keys_out), (values_t, values_out)], sems.at[pl.ds(0, 2)])
    copies[3 + pieces].wait()
    copies[4 + pieces].wait()
    row = gain_row(hbuf)
    copies[5 + pieces].wait()
    for piece in norm_pieces(lbuf.at[0], row, xbuf):
        piece()
    project_query(xbuf, wq, qbuf.at[0])
    for i, out in enumerate(outs):
        todo = []
        if i + 1 < len(outs):
            copies[6 + pieces + i].wait()
            todo = norm_pieces(lbuf.at[i + 1], row, xbuf)

        def between():
            if todo:
                todo.pop(0)()

        attend_chunk(qbuf.at[i % 2], keys, values_t, sbuf, pbuf, nbuf, out, between)
        if i + 1 < len(outs):
            for piece in todo:
                piece()
            project_query(xbuf, wq, qbuf.at[(i + 1) % 2])
    for copy in back:
        copy.wait()


def own_kernel(
    where, latents, gain, wq_in, keys_in, values_in, out,
    lbuf, gbuf, wq, keys, values_t, xbuf, qbuf, sbuf, pbuf, nbuf, sems,
):
    nz = lbuf.shape[0]
    copies = fetch(
        [(gain, gbuf), (latents.at[:, where[0]], lbuf), (wq_in, wq), (keys_in, keys), (values_in, values_t)],
        sems,
    )
    copies[0].wait()
    row = gain_row(gbuf)
    copies[1].wait()
    for piece in norm_pieces(lbuf, row, xbuf):
        piece()
    copies[2].wait()
    project_query(xbuf, wq, qbuf)
    copies[3].wait()
    copies[4].wait()
    attend_chunk(qbuf, keys, values_t, sbuf, pbuf, nbuf, out, lambda: None)


def anywhere():
    return pl.BlockSpec(memory_space=pl.ANY)


def whole():
    return pl.BlockSpec(memory_space=pltpu.VMEM)


def anywhere():
    return pl.BlockSpec(memory_space=pl.ANY)


def attend_scratch(n):
    return [
        pltpu.VMEM((2, CHUNK, LANES), F32),
        pltpu.VMEM((2, n, LANES), BF16),
        pltpu.VMEM((2, AUG, LANES), BF16),
    ]


def encode_call(where, points, latents, gain_in, gain_lat, wk, wv, wq):
    n, width = points.shape
    nz, nx, rows, depth = latents.shape
    part = jax.ShapeDtypeStruct((nz, AUG, 2 * rows), BF16)
    keys = jax.ShapeDtypeStruct((n, 2 * HS), BF16)
    values_t = jax.ShapeDtypeStruct((2, AUG, n), BF16)
    return pl.pallas_call(
        encode_kernel,
        out_shape=(part, part, part, keys, values_t),
        in_specs=[pl.BlockSpec(memory_space=pltpu.SMEM)] + [anywhere()] * 7,
        out_specs=(whole(), whole(), whole(), anywhere(), anywhere()),
        scratch_shapes=[
            pltpu.VMEM(points.shape, BF16),
            pltpu.VMEM((nx - 1, nz, rows, depth), BF16),
            pltpu.VMEM(gain_in.shape, F32),
            pltpu.VMEM(gain_lat.shape, F32),
            pltpu.VMEM(wk.shape, BF16),
            pltpu.VMEM(wv.shape, BF16),
            pltpu.VMEM(wq.shape, BF16),
            pltpu.VMEM(keys.shape, BF16),
            pltpu.VMEM(values_t.shape, BF16),
            pltpu.VMEM((PIECE, width), BF16),
            pltpu.VMEM((nz * rows, depth), BF16),
            pltpu.VMEM((2, nz * rows, 2 * HS), BF16),
        ]
        + attend_scratch(n)
        + [pltpu.SemaphoreType.DMA((n // PIECE + 8,))],
        compiler_params=pltpu.CompilerParams(vmem_limit_bytes=VMEM_WIDE),
        cost_estimate=pl.CostEstimate(
            flops=16 * 10**9, bytes_accessed=10**7, transcendentals=6 * 10**6
        ),
        name="encode",
    )(where, points, latents, gain_in, gain_lat, wk, wv, wq)


def own_call(where, latents, gain, wq, keys, values_t):
    nz, nx, rows, depth = latents.shape
    return pl.pallas_call(
        own_kernel,
        out_shape=jax.ShapeDtypeStruct((nz, AUG, 2 * rows), BF16),
        in_specs=[pl.BlockSpec(memory_space=pltpu.SMEM)] + [anywhere()] * 5,
        out_specs=whole(),
        scratch_shapes=[
            pltpu.VMEM((nz, rows, depth), BF16),
            pltpu.VMEM(gain.shape, F32),
            pltpu.VMEM(wq.shape, BF16),
            pltpu.VMEM(keys.shape, BF16),
            pltpu.VMEM(values_t.shape, BF16),
            pltpu.VMEM((nz * rows, depth), BF16),
            pltpu.VMEM((nz * rows, 2 * HS), BF16),
        ]
        + attend_scratch(keys.shape[0])
        + [pltpu.SemaphoreType.DMA((5,))],
        compiler_params=pltpu.CompilerParams(vmem_limit_bytes=VMEM_WIDE),
        cost_estimate=pl.CostEstimate(
            flops=4 * 10**9, bytes_accessed=5 * 10**6, transcendentals=2 * 10**6
        ),
        name="own",
    )(where, latents, gain, wq, keys, values_t)


def merge(parts):
    shifts = [p[HS + 2 : HS + 3] + p[HS + 3 : HS + 4] for p in parts]
    high, low = split_pair(functools.reduce(jnp.maximum, shifts))
    top = high + low
    acc = functools.reduce(jnp.add, [p * jnp.exp2(s - top) for p, s in zip(parts, shifts)])
    return acc, acc[HS : HS + 1] + acc[HS + 1 : HS + 2], high, low


def combine_kernel(a, b, c, d, out):
    for z in range(a.shape[0]):
        acc, total, high, low = merge([r[z].astype(F32) for r in (a, b, c, d)])
        out[z] = with_stats(acc, total, high, low)


def finish_kernel(*refs):
    out = refs[-1]
    parts = [r[i].astype(F32) for r in refs[:-1] for i in range(r.shape[0])]
    acc, total, _, _ = merge(parts)
    rows = out.shape[0]
    value = (acc[:HS] / total).T
    out[...] = jnp.concatenate([value[:rows], value[rows:]], axis=1).astype(BF16)


def near_kernel(a0, a1, a2, a3, w0, w1, w2, w3, out):
    total = None
    for a, w in ((a0, w0), (a1, w1), (a2, w2), (a3, w3)):
        term = jnp.dot(a[...], w[...], preferred_element_type=F32)
        total = term if total is None else total + term
    out[...] = total


def middle_kernel(latents, gain, own, other, wq, wk, wv, mid, q, kv):
    total = latents[...].astype(F32) + (own[...] + other[...])
    mid[...] = total
    x = normed(total, gain_row(gain))
    q[...] = lax.dot_general(x, wq[...], NT, preferred_element_type=F32).astype(BF16)
    k = lax.dot_general(x, wk[...], NT, preferred_element_type=F32).astype(BF16)
    v = lax.dot_general(x, wv[...], NT, preferred_element_type=F32).astype(BF16)
    both = jnp.concatenate([k, v], axis=1)
    for i in range(kv.shape[0]):
        kv[i] = both


def self_kernel(kv, q0, q1, q2, q3, out):
    scale = LOG2E * HS ** (-0.5)
    width = 2 * HS
    rows = q0.shape[0]
    keys = kv[:, 0:width]
    values_t = kv[:, width : 2 * width].astype(F32).T.astype(BF16)
    lane = lax.broadcasted_iota(jnp.int32, (rows, width), 1)
    first = lax.broadcasted_iota(jnp.int32, (HS, 2 * rows), 1) < rows
    for i, ref in enumerate((q0, q1, q2, q3)):
        q = ref[...]
        zero = jnp.zeros_like(q)
        both = jnp.concatenate([jnp.where(lane < HS, q, zero), jnp.where(lane < HS, zero, q)], axis=0)
        s = lax.dot_general(keys, both, NT, preferred_element_type=F32) * scale
        high, low = split_pair(jnp.max(s, axis=0, keepdims=True))
        p = jnp.exp2(s - (high + low))
        total = jnp.sum(p, axis=0, keepdims=True)
        n = jnp.dot(values_t, p.astype(BF16), preferred_element_type=F32)
        out[i] = with_stats(jnp.where(first, n[:HS], n[HS:]), total, high, low)


def output_kernel(where, a0, a1, a2, a3, w, own, other):
    rows, width = a0.shape
    total = None
    for i, a in enumerate((a0, a1, a2, a3)):
        term = jnp.dot(a[...], w[i * width : (i + 1) * width, :], preferred_element_type=F32)
        total = term if total is None else total + term
    left, right = total[:, :width], total[:, width:]
    mine = where[0] == 0
    own[...] = jnp.where(mine, left, right)
    other[...] = jnp.where(mine, right, left)


def add_kernel(mid, own, other, out):
    out[...] = (mid[...] + (own[...] + other[...])).astype(BF16)


def plain_call(kernel, name, out_shape, *args, flops=10**8):
    moved = sum(a.size * a.dtype.itemsize for a in args)
    spec = lambda a: pl.BlockSpec(memory_space=pltpu.SMEM) if a.dtype == jnp.int32 else whole()
    return pl.pallas_call(
        kernel,
        out_shape=out_shape,
        in_specs=[spec(a) for a in args],
        out_specs=jax.tree.map(lambda _: whole(), out_shape),
        compiler_params=pltpu.CompilerParams(vmem_limit_bytes=VMEM_LIMIT),
        cost_estimate=pl.CostEstimate(flops=flops, bytes_accessed=moved, transcendentals=0),
        name=name,
    )(*args)


def permute_x(v, k):
    return lax.ppermute(
        v, "seq", [(i, (i // NX) * NX + (i % NX + k) % NX) for i in range(NX * NZ)]
    )


def permute_y(v, k):
    return lax.ppermute(v, "head", [(i, (i + 2 * k) % (2 * NY)) for i in range(2 * NY)])


def swap_cores(v):
    return lax.ppermute(v, "head", [(i, i ^ 1) for i in range(2 * NY)])


def gather_y(v):
    return [v] + [permute_y(v, k) for k in SHIFTS]


def body(
    points,
    latents,
    gain_in,
    gain_lat,
    gain_self,
    cross_query,
    cross_key,
    cross_value,
    cross_out,
    self_query,
    latent_key_weight,
    self_value,
    self_out,
):
    width = cross_query.shape[1]
    count, depth = latents.shape
    rows = count // (NX * NZ)
    seq = lax.axis_index("seq").astype(jnp.int32)
    head = lax.axis_index("head").astype(jnp.int32)
    part_shape = jax.ShapeDtypeStruct((NZ, AUG, 2 * rows), BF16)
    gains = [g.reshape(-1, 128) for g in (gain_in, gain_lat, gain_self)]

    pair = 2 * width
    y, core = head // 2, head % 2
    mine = [
        lax.dynamic_slice_in_dim(self_out, ((y + k) % NY) * pair, pair, 1) for k in (0,) + SHIFTS
    ]
    mine = [mine[0]] + [permute_y(v, k) for v, k in zip(mine[1:], SHIFTS)]
    out_near = [cross_out] + [permute_y(cross_out, k) for k in SHIFTS[:2]]
    latents_4d = latents.reshape(NZ, NX, rows, depth)
    x = (seq % NX).reshape(1)
    *sent, keys, values_t = encode_call(
        x, points, latents_4d, gains[0], gains[1], cross_key.T, cross_value.T, cross_query.T
    )
    parts = [permute_x(v, k) for v, k in zip(sent, FOREIGN)]
    keys, mine, last = lax.optimization_barrier((keys, mine, cross_out))
    out_near.append(permute_y(last, SHIFTS[2]))
    mine = jnp.concatenate(mine, axis=0)
    part = own_call(x, latents_4d, gains[1], cross_query.T, keys, values_t)
    part = plain_call(combine_kernel, "combine", part_shape, part, *parts)
    lat_rows = lax.dynamic_slice_in_dim(latents, seq * rows, rows, 0)
    part = lax.all_to_all(part, "seq", 0, 0, axis_index_groups=Z_GROUPS)
    part, mine, out_near, lat_rows = lax.optimization_barrier((part, mine, out_near, lat_rows))
    block = jax.ShapeDtypeStruct((rows, width), BF16)
    cross_attn = plain_call(finish_kernel, "finish", block, part)
    own = plain_call(
        near_kernel, "near", jax.ShapeDtypeStruct((rows, depth), F32), *gather_y(cross_attn), *out_near
    )
    mid, squery, kv = plain_call(
        middle_kernel, "middle",
        (
            jax.ShapeDtypeStruct((rows, depth), F32),
            block,
            jax.ShapeDtypeStruct((NZ, rows, pair), BF16),
        ),
        lat_rows, gains[2], own, swap_cores(own),
        self_query.T, latent_key_weight.T, self_value.T,
    )
    kv = lax.all_to_all(kv, "seq", 0, 0, axis_index_groups=Z_GROUPS)
    squeries = [squery] + [permute_x(squery, k) for k in SHIFTS]
    mid_cols = lax.dynamic_slice_in_dim(mid, head * width, width, 1)
    kv, mid_cols = lax.optimization_barrier((kv, mid_cols))
    part = plain_call(
        self_kernel, "self_part", jax.ShapeDtypeStruct((NX, AUG, 2 * rows), BF16),
        kv.reshape(NZ * rows, pair), *squeries,
    )
    back = [part[0:1]] + [permute_x(part[i + 1 : i + 2], -k) for i, k in enumerate(SHIFTS)]
    self_attn = plain_call(finish_kernel, "finish_self", block, *back)
    half = jax.ShapeDtypeStruct((rows, width), F32)
    own, give = plain_call(
        output_kernel, "output", (half, half), core.reshape(1), *gather_y(self_attn), mine
    )
    return plain_call(add_kernel, "add", block, mid_cols, own, swap_cores(give))


def solution(mesh):
    in_specs = (
        P("seq", None),
        P(),
        P(),
        P(),
        P(),
        P(None, "head"),
        P(None, "head"),
        P(None, "head"),
        P("head", None),
        P(None, "head"),
        P(None, "head"),
        P(None, "head"),
        P("head", None),
    )
    out_specs = P("seq", "head")
    return jax.shard_map(body, mesh=mesh, in_specs=in_specs, out_specs=out_specs, check_vma=False)
```

```python
import functools
import jax
import jax.numpy as jnp
from jax import lax
from jax.experimental import pallas as pl
from jax.experimental.pallas import tpu as pltpu
from jax.sharding import PartitionSpec as P

NX = 4
NY = 4
NZ = 8
Z_GROUPS = [[z * NX + x for z in range(NZ)] for x in range(NX)]
SHIFTS = (1, NX - 1, 2)
FOREIGN = (2, 1, NX - 1)

HS = 96
AUG = 112
LANES = 256
CHUNK = 256
PIECE = 512
LOG2E = 1.4426950408889634
SAFE = 2.0**64
F32 = jnp.float32
BF16 = jnp.bfloat16
NT = (((1,), (1,)), ((), ()))
VMEM_LIMIT = 20 * 1024 * 1024
VMEM_WIDE = 58 * 1024 * 1024


def normed(values, gain):
    values = values.astype(F32)
    center = values - jnp.mean(values, axis=-1, keepdims=True)
    spread = jnp.mean(center * center, axis=-1, keepdims=True)
    return (center * lax.rsqrt(spread + 1e-05) * gain).astype(BF16)


def gain_row(gain):
    return jnp.concatenate([gain[i : i + 1, :] for i in range(gain.shape[0])], axis=1)


def split_pair(value):
    high = value.astype(BF16).astype(F32)
    return high, (value - high).astype(BF16).astype(F32)


def fetch(pairs, sems):
    return [pltpu.make_async_copy(src, dst, sems.at[i]) for i, (src, dst) in enumerate(pairs)]


def project_points(pbuf, gain, wk, wv, keys, values_t, xbuf, ready):
    one = (lax.broadcasted_iota(jnp.int32, (AUG - HS, PIECE), 0) == 0).astype(BF16)
    for i in range(pbuf.shape[0] // PIECE):
        ready(i)
        row = gain_row(gain)
        rows = pl.ds(i * PIECE, PIECE)
        for j in range(0, PIECE, 64):
            xbuf[j : j + 64, :] = normed(pbuf[i * PIECE + j : i * PIECE + j + 64, :], row)
        x = xbuf[...]
        keys[rows, :] = lax.dot_general(x, wk[...], NT, preferred_element_type=F32).astype(BF16)
        vt = lax.dot_general(wv[...], x, NT, preferred_element_type=F32).astype(BF16)
        for h in range(2):
            values_t[h, 0:HS, rows] = vt[h * HS : (h + 1) * HS]
            values_t[h, HS:AUG, rows] = one


def attend_units(queries, keys, values_t, sbuf, pbuf, emit):
    count = keys.shape[0]
    scale = LOG2E * HS ** (-0.5)
    chunks = count // CHUNK

    def score(u, c):
        rows = pl.ds(c * CHUNK, CHUNK)
        return lax.dot_general(keys[rows, :], queries[u][1], NT, preferred_element_type=F32)

    def first(u):
        s = score(u, 0)
        sbuf[u % 2] = s
        return split_pair(jnp.max(s, axis=0, keepdims=True) * scale)

    largest = jnp.zeros((1, LANES), F32)
    state = first(0)
    for u, (h, q) in enumerate(queries):
        high, low = state
        shift = high + low
        for c in range(chunks):
            s = sbuf[u % 2] if c == 0 else score(u, c)
            pbuf[u % 2, c * CHUNK : (c + 1) * CHUNK, :] = jnp.exp2(s * scale - shift).astype(BF16)
        acc = jnp.dot(values_t[h], pbuf[u % 2], preferred_element_type=F32)
        if u + 1 < len(queries):
            state = first(u + 1)
        emit(u, acc, high, low)
        largest = jnp.maximum(largest, acc[HS : HS + 1])
    return jnp.max(largest)


def attend_exact(h, q, keys, values_t):
    scale = LOG2E * HS ** (-0.5)
    chunks = keys.shape[0] // CHUNK

    def scores(c):
        rows = pl.ds(pl.multiple_of(c * CHUNK, CHUNK), CHUNK)
        s = lax.dot_general(keys[rows, :], q, NT, preferred_element_type=F32)
        return s * scale

    def largest(c, top):
        return jnp.maximum(top, jnp.max(scores(c), axis=0, keepdims=True))

    top = lax.fori_loop(0, chunks, largest, jnp.full((1, LANES), -jnp.inf, F32))
    high, low = split_pair(top)
    shift = high + low

    def add(c, acc):
        rows = pl.ds(pl.multiple_of(c * CHUNK, CHUNK), CHUNK)
        p = jnp.exp2(scores(c) - shift).astype(BF16)
        return acc + jnp.dot(values_t[h, :, rows], p, preferred_element_type=F32)

    acc = lax.fori_loop(0, chunks, add, jnp.zeros((AUG, LANES), F32))
    return acc, high, low


def with_stats(acc, total, high, low):
    total_high, total_low = split_pair(total)
    row = lax.broadcasted_iota(jnp.int32, (AUG - HS, acc.shape[1]), 0)
    stats = jnp.where(row == 0, total_high, 0.0)
    stats = jnp.where(row == 1, total_low, stats)
    stats = jnp.where(row == 2, high, stats)
    stats = jnp.where(row == 3, low, stats)
    return jnp.concatenate([acc[:HS], stats], axis=0).astype(BF16)


def attend_chunk(qbuf, keys, values_t, sbuf, pbuf, nbuf, out):
    rows = out.shape[2] // 2
    blocks = qbuf.shape[0] // LANES
    per = LANES // rows

    def query(j, h):
        start = j * LANES if isinstance(j, int) else pl.multiple_of(j * LANES, LANES)
        q = qbuf[pl.ds(start, LANES), :]
        lane = lax.broadcasted_iota(jnp.int32, q.shape, 1)
        return jnp.where((lane < HS) == (h == 0), q, jnp.zeros_like(q))

    def emit_at(j, h, acc, high, low):
        nbuf[h] = with_stats(acc, acc[HS : HS + 1], high, low)
        if h == 1:
            for i in range(per):
                lanes = slice(i * rows, (i + 1) * rows)
                out[j * per + i] = jnp.concatenate([nbuf[0, :, lanes], nbuf[1, :, lanes]], axis=1)

    queries = [(h, query(j, h)) for j in range(blocks) for h in range(2)]
    above = attend_units(
        queries, keys, values_t, sbuf, pbuf, lambda u, *r: emit_at(u // 2, u % 2, *r)
    )

    @pl.when(jnp.logical_not(above <= SAFE))
    def _():
        def again(j, carry):
            for h in range(2):
                emit_at(j, h, *attend_exact(h, query(j, h), keys, values_t))
            return carry

        lax.fori_loop(0, blocks, again, 0)


def norm_rows(lbuf, row, xbuf):
    rows = lbuf.shape[1]
    for z in range(lbuf.shape[0]):
        xbuf[z * rows : (z + 1) * rows, :] = normed(lbuf[z], row)


def project_query(xbuf, wq, qbuf):
    qbuf[...] = lax.dot_general(xbuf[...], wq[...], NT, preferred_element_type=F32).astype(BF16)


def encode_kernel(
    where, points, latents, gain_in, gain_lat, wk_in, wv_in, wq_in,
    out0, out1, out2, keys_out, values_out,
    pts, lbuf, gbuf, hbuf, wk, wv, wq, keys, values_t, ybuf, xbuf, qbuf, sbuf, pbuf, nbuf, sems,
):
    outs = (out0, out1, out2)
    pieces = [pl.ds(i * PIECE, PIECE) for i in range(pts.shape[0] // PIECE)]
    first = fetch(
        [(points.at[pieces[0], :], pts.at[pieces[0], :]), (gain_in, gbuf), (wk_in, wk), (wv_in, wv)]
        + [(points.at[rows, :], pts.at[rows, :]) for rows in pieces[1:]],
        sems,
    )
    later = fetch(
        [(gain_lat, hbuf), (wq_in, wq)]
        + [(latents.at[:, lax.rem(where[0] + k, NX)], lbuf.at[i]) for i, k in enumerate(FOREIGN)],
        sems.at[pl.ds(len(first), len(outs) + 2)],
    )
    back = fetch([(keys, keys_out), (values_t, values_out)], sems.at[pl.ds(0, 2)])
    for copy in first:
        copy.start()

    def ready(i):
        if i == 0:
            for copy in first[:4]:
                copy.wait()
            for copy in later:
                copy.start()
        else:
            first[3 + i].wait()

    project_points(pts, gbuf, wk, wv, keys, values_t, ybuf, ready)
    for copy in back:
        copy.start()
    later[0].wait()
    later[1].wait()
    row = gain_row(hbuf)
    for i, out in enumerate(outs):
        later[2 + i].wait()
        norm_rows(lbuf.at[i], row, xbuf)
        project_query(xbuf, wq, qbuf)
        attend_chunk(qbuf, keys, values_t, sbuf, pbuf, nbuf, out)
    for copy in back:
        copy.wait()


def own_kernel(
    where, latents, gain, wq_in, keys_in, values_in, out,
    lbuf, gbuf, wq, keys, values_t, xbuf, qbuf, sbuf, pbuf, nbuf, sems,
):
    copies = fetch(
        [(latents.at[:, where[0]], lbuf), (gain, gbuf), (wq_in, wq), (keys_in, keys), (values_in, values_t)],
        sems,
    )
    for copy in copies:
        copy.start()
    copies[0].wait()
    copies[1].wait()
    norm_rows(lbuf, gain_row(gbuf), xbuf)
    copies[2].wait()
    project_query(xbuf, wq, qbuf)
    copies[3].wait()
    copies[4].wait()
    attend_chunk(qbuf, keys, values_t, sbuf, pbuf, nbuf, out)


def anywhere():
    return pl.BlockSpec(memory_space=pl.ANY)


def whole():
    return pl.BlockSpec(memory_space=pltpu.VMEM)


def anywhere():
    return pl.BlockSpec(memory_space=pl.ANY)


def attend_scratch(n):
    return [
        pltpu.VMEM((2, CHUNK, LANES), F32),
        pltpu.VMEM((2, n, LANES), BF16),
        pltpu.VMEM((2, AUG, LANES), BF16),
    ]


def encode_call(where, points, latents, gain_in, gain_lat, wk, wv, wq):
    n, width = points.shape
    nz, nx, rows, depth = latents.shape
    part = jax.ShapeDtypeStruct((nz, AUG, 2 * rows), BF16)
    keys = jax.ShapeDtypeStruct((n, 2 * HS), BF16)
    values_t = jax.ShapeDtypeStruct((2, AUG, n), BF16)
    return pl.pallas_call(
        encode_kernel,
        out_shape=(part, part, part, keys, values_t),
        in_specs=[pl.BlockSpec(memory_space=pltpu.SMEM)] + [anywhere()] * 7,
        out_specs=(whole(), whole(), whole(), anywhere(), anywhere()),
        scratch_shapes=[
            pltpu.VMEM(points.shape, BF16),
            pltpu.VMEM((nx - 1, nz, rows, depth), BF16),
            pltpu.VMEM(gain_in.shape, F32),
            pltpu.VMEM(gain_lat.shape, F32),
            pltpu.VMEM(wk.shape, BF16),
            pltpu.VMEM(wv.shape, BF16),
            pltpu.VMEM(wq.shape, BF16),
            pltpu.VMEM(keys.shape, BF16),
            pltpu.VMEM(values_t.shape, BF16),
            pltpu.VMEM((PIECE, width), BF16),
            pltpu.VMEM((nz * rows, depth), BF16),
            pltpu.VMEM((nz * rows, 2 * HS), BF16),
        ]
        + attend_scratch(n)
        + [pltpu.SemaphoreType.DMA((n // PIECE + 8,))],
        compiler_params=pltpu.CompilerParams(vmem_limit_bytes=VMEM_WIDE),
        cost_estimate=pl.CostEstimate(
            flops=16 * 10**9, bytes_accessed=10**7, transcendentals=6 * 10**6
        ),
        name="encode",
    )(where, points, latents, gain_in, gain_lat, wk, wv, wq)


def own_call(where, latents, gain, wq, keys, values_t):
    nz, nx, rows, depth = latents.shape
    return pl.pallas_call(
        own_kernel,
        out_shape=jax.ShapeDtypeStruct((nz, AUG, 2 * rows), BF16),
        in_specs=[pl.BlockSpec(memory_space=pltpu.SMEM)] + [anywhere()] * 5,
        out_specs=whole(),
        scratch_shapes=[
            pltpu.VMEM((nz, rows, depth), BF16),
            pltpu.VMEM(gain.shape, F32),
            pltpu.VMEM(wq.shape, BF16),
            pltpu.VMEM(keys.shape, BF16),
            pltpu.VMEM(values_t.shape, BF16),
            pltpu.VMEM((nz * rows, depth), BF16),
            pltpu.VMEM((nz * rows, 2 * HS), BF16),
        ]
        + attend_scratch(keys.shape[0])
        + [pltpu.SemaphoreType.DMA((5,))],
        compiler_params=pltpu.CompilerParams(vmem_limit_bytes=VMEM_WIDE),
        cost_estimate=pl.CostEstimate(
            flops=4 * 10**9, bytes_accessed=5 * 10**6, transcendentals=2 * 10**6
        ),
        name="own",
    )(where, latents, gain, wq, keys, values_t)


def merge(parts):
    shifts = [p[HS + 2 : HS + 3] + p[HS + 3 : HS + 4] for p in parts]
    high, low = split_pair(functools.reduce(jnp.maximum, shifts))
    top = high + low
    acc = functools.reduce(jnp.add, [p * jnp.exp2(s - top) for p, s in zip(parts, shifts)])
    return acc, acc[HS : HS + 1] + acc[HS + 1 : HS + 2], high, low


def combine_kernel(a, b, c, d, out):
    for z in range(a.shape[0]):
        acc, total, high, low = merge([r[z].astype(F32) for r in (a, b, c, d)])
        out[z] = with_stats(acc, total, high, low)


def finish_kernel(*refs):
    out = refs[-1]
    parts = [r[i].astype(F32) for r in refs[:-1] for i in range(r.shape[0])]
    acc, total, _, _ = merge(parts)
    rows = out.shape[0]
    value = (acc[:HS] / total).T
    out[...] = jnp.concatenate([value[:rows], value[rows:]], axis=1).astype(BF16)


def near_kernel(a0, a1, a2, a3, w0, w1, w2, w3, out):
    total = None
    for a, w in ((a0, w0), (a1, w1), (a2, w2), (a3, w3)):
        term = jnp.dot(a[...], w[...], preferred_element_type=F32)
        total = term if total is None else total + term
    out[...] = total


def middle_kernel(latents, gain, own, other, wq, wk, wv, mid, q, kv):
    total = latents[...].astype(F32) + (own[...] + other[...])
    mid[...] = total
    x = normed(total, gain_row(gain))
    q[...] = lax.dot_general(x, wq[...], NT, preferred_element_type=F32).astype(BF16)
    k = lax.dot_general(x, wk[...], NT, preferred_element_type=F32).astype(BF16)
    v = lax.dot_general(x, wv[...], NT, preferred_element_type=F32).astype(BF16)
    both = jnp.concatenate([k, v], axis=1)
    for i in range(kv.shape[0]):
        kv[i] = both


def self_kernel(kv, q0, q1, q2, q3, out):
    scale = LOG2E * HS ** (-0.5)
    width = 2 * HS
    rows = q0.shape[0]
    keys = kv[:, 0:width]
    values_t = kv[:, width : 2 * width].astype(F32).T.astype(BF16)
    lane = lax.broadcasted_iota(jnp.int32, (rows, width), 1)
    first = lax.broadcasted_iota(jnp.int32, (HS, 2 * rows), 1) < rows
    for i, ref in enumerate((q0, q1, q2, q3)):
        q = ref[...]
        zero = jnp.zeros_like(q)
        both = jnp.concatenate([jnp.where(lane < HS, q, zero), jnp.where(lane < HS, zero, q)], axis=0)
        s = lax.dot_general(keys, both, NT, preferred_element_type=F32) * scale
        high, low = split_pair(jnp.max(s, axis=0, keepdims=True))
        p = jnp.exp2(s - (high + low))
        total = jnp.sum(p, axis=0, keepdims=True)
        n = jnp.dot(values_t, p.astype(BF16), preferred_element_type=F32)
        out[i] = with_stats(jnp.where(first, n[:HS], n[HS:]), total, high, low)


def output_kernel(attn, w, out):
    width = attn.shape[1]
    terms = jnp.dot(attn[...], w[...], preferred_element_type=F32)
    for i in range(out.shape[0]):
        out[i] = terms[:, i * width : (i + 1) * width].astype(BF16)


def add_kernel(mid, terms, out):
    total = mid[...]
    for i in range(terms.shape[0]):
        total = total + terms[i].astype(F32)
    out[...] = total.astype(BF16)


def plain_call(kernel, name, out_shape, *args, flops=6 * 10**9):
    moved = sum(a.size * a.dtype.itemsize for a in args)
    spec = lambda a: pl.BlockSpec(memory_space=pltpu.SMEM) if a.dtype == jnp.int32 else whole()
    return pl.pallas_call(
        kernel,
        out_shape=out_shape,
        in_specs=[spec(a) for a in args],
        out_specs=jax.tree.map(lambda _: whole(), out_shape),
        compiler_params=pltpu.CompilerParams(vmem_limit_bytes=VMEM_LIMIT),
        cost_estimate=pl.CostEstimate(flops=flops, bytes_accessed=moved, transcendentals=0),
        name=name,
    )(*args)


def permute_x(v, k):
    return lax.ppermute(
        v, "seq", [(i, (i // NX) * NX + (i % NX + k) % NX) for i in range(NX * NZ)]
    )


def permute_y(v, k):
    return lax.ppermute(v, "head", [(i, (i + 2 * k) % (2 * NY)) for i in range(2 * NY)])


def swap_cores(v):
    return lax.ppermute(v, "head", [(i, i ^ 1) for i in range(2 * NY)])


def gather_y(v):
    return [v] + [permute_y(v, k) for k in SHIFTS]


def body(
    points,
    latents,
    gain_in,
    gain_lat,
    gain_self,
    cross_query,
    cross_key,
    cross_value,
    cross_out,
    self_query,
    latent_key_weight,
    self_value,
    self_out,
):
    width = cross_query.shape[1]
    count, depth = latents.shape
    rows = count // (NX * NZ)
    seq = lax.axis_index("seq").astype(jnp.int32)
    head = lax.axis_index("head").astype(jnp.int32)
    part_shape = jax.ShapeDtypeStruct((NZ, AUG, 2 * rows), BF16)
    gains = [g.reshape(-1, 128) for g in (gain_in, gain_lat, gain_self)]

    out_near = gather_y(cross_out)
    latents_4d = latents.reshape(NZ, NX, rows, depth)
    x = (seq % NX).reshape(1)
    *sent, keys, values_t = encode_call(
        x, points, latents_4d, gains[0], gains[1], cross_key.T, cross_value.T, cross_query.T
    )
    parts = [permute_x(v, k) for v, k in zip(sent, FOREIGN)]
    part = own_call(x, latents_4d, gains[1], cross_query.T, keys, values_t)
    part = plain_call(combine_kernel, "combine", part_shape, part, *parts)
    lat_rows = lax.dynamic_slice_in_dim(latents, seq * rows, rows, 0)
    part = lax.all_to_all(part, "seq", 0, 0, axis_index_groups=Z_GROUPS)
    part, out_near, lat_rows = lax.optimization_barrier((part, out_near, lat_rows))
    block = jax.ShapeDtypeStruct((rows, width), BF16)
    cross_attn = plain_call(finish_kernel, "finish", block, part)
    own = plain_call(
        near_kernel, "near", jax.ShapeDtypeStruct((rows, depth), F32), *gather_y(cross_attn), *out_near
    )
    mid, squery, kv = plain_call(
        middle_kernel, "middle",
        (
            jax.ShapeDtypeStruct((rows, depth), F32),
            block,
            jax.ShapeDtypeStruct((NZ, rows, 2 * width), BF16),
        ),
        lat_rows, gains[2], own, swap_cores(own),
        self_query.T, latent_key_weight.T, self_value.T,
    )
    kv = lax.all_to_all(kv, "seq", 0, 0, axis_index_groups=Z_GROUPS)
    squeries = [squery] + [permute_x(squery, k) for k in SHIFTS]
    mid_cols = lax.dynamic_slice_in_dim(mid, head * width, width, 1)
    kv, mid_cols = lax.optimization_barrier((kv, mid_cols))
    part = plain_call(
        self_kernel, "self_part", jax.ShapeDtypeStruct((NX, AUG, 2 * rows), BF16),
        kv.reshape(NZ * rows, 2 * width), *squeries,
    )
    back = [part[0:1]] + [permute_x(part[i + 1 : i + 2], -k) for i, k in enumerate(SHIFTS)]
    self_attn = plain_call(finish_kernel, "finish_self", block, *back)
    terms = plain_call(
        output_kernel, "output", jax.ShapeDtypeStruct((2 * NY, rows, width), BF16), self_attn, self_out
    )
    terms = lax.all_to_all(terms, "head", 0, 0)
    return plain_call(add_kernel, "add", block, mid_cols, terms)


def solution(mesh):
    in_specs = (
        P("seq", None),
        P(),
        P(),
        P(),
        P(),
        P(None, "head"),
        P(None, "head"),
        P(None, "head"),
        P("head", None),
        P(None, "head"),
        P(None, "head"),
        P(None, "head"),
        P("head", None),
    )
    out_specs = P("seq", "head")
    return jax.shard_map(body, mesh=mesh, in_specs=in_specs, out_specs=out_specs, check_vma=False)
```

```python
import functools
import jax
import jax.numpy as jnp
from jax import lax
from jax.experimental import pallas as pl
from jax.experimental.pallas import tpu as pltpu
from jax.sharding import PartitionSpec as P

NX = 4
NY = 4
NZ = 8
Z_GROUPS = [[z * NX + x for z in range(NZ)] for x in range(NX)]
SHIFTS = (1, NX - 1, 2)
FOREIGN = (2, 1, NX - 1)

HS = 96
AUG = 112
LANES = 256
CHUNK = 256
PIECE = 512
LOG2E = 1.4426950408889634
SAFE = 2.0**64
F32 = jnp.float32
BF16 = jnp.bfloat16
NT = (((1,), (1,)), ((), ()))
VMEM_LIMIT = 20 * 1024 * 1024
VMEM_WIDE = 58 * 1024 * 1024


def normed(values, gain):
    values = values.astype(F32)
    center = values - jnp.mean(values, axis=-1, keepdims=True)
    spread = jnp.mean(center * center, axis=-1, keepdims=True)
    return (center * lax.rsqrt(spread + 1e-05) * gain).astype(BF16)


def gain_row(gain):
    return jnp.concatenate([gain[i : i + 1, :] for i in range(gain.shape[0])], axis=1)


def split_pair(value):
    high = value.astype(BF16).astype(F32)
    return high, (value - high).astype(BF16).astype(F32)


def fetch(pairs, sems):
    return [pltpu.make_async_copy(src, dst, sems.at[i]) for i, (src, dst) in enumerate(pairs)]


def project_points(pbuf, gain, wk, wv, keys, values_t, xbuf, ready):
    for i in range(pbuf.shape[0] // PIECE):
        ready(i)
        row = gain_row(gain)
        for j in range(i * PIECE, (i + 1) * PIECE, 64):
            xbuf[j : j + 64, :] = normed(pbuf[j : j + 64, :], row)
    x = xbuf[...]
    keys[...] = lax.dot_general(x, wk[...], NT, preferred_element_type=F32).astype(BF16)
    vt = lax.dot_general(wv[...], x, NT, preferred_element_type=F32).astype(BF16)
    for h in range(2):
        values_t[h, 0:HS, :] = vt[h * HS : (h + 1) * HS]
    one = lax.broadcasted_iota(jnp.int32, (AUG - HS, pbuf.shape[0]), 0) == 0
    for h in range(2):
        values_t[h, HS:AUG, :] = one.astype(BF16)


def attend_units(queries, keys, values_t, sbuf, pbuf, emit):
    count = keys.shape[0]
    scale = LOG2E * HS ** (-0.5)
    chunks = count // CHUNK

    def score(u, c):
        rows = pl.ds(c * CHUNK, CHUNK)
        return lax.dot_general(keys[rows, :], queries[u][1], NT, preferred_element_type=F32)

    def first(u):
        s = score(u, 0)
        sbuf[u % 2] = s
        return split_pair(jnp.max(s, axis=0, keepdims=True) * scale)

    largest = jnp.zeros((1, LANES), F32)
    state = first(0)
    for u, (h, q) in enumerate(queries):
        high, low = state
        shift = high + low
        for c in range(chunks):
            s = sbuf[u % 2] if c == 0 else score(u, c)
            pbuf[u % 2, c * CHUNK : (c + 1) * CHUNK, :] = jnp.exp2(s * scale - shift).astype(BF16)
        acc = jnp.dot(values_t[h], pbuf[u % 2], preferred_element_type=F32)
        if u + 1 < len(queries):
            state = first(u + 1)
        emit(u, acc, high, low)
        largest = jnp.maximum(largest, acc[HS : HS + 1])
    return jnp.max(largest)


def attend_exact(h, q, keys, values_t):
    scale = LOG2E * HS ** (-0.5)
    chunks = keys.shape[0] // CHUNK

    def scores(c):
        rows = pl.ds(pl.multiple_of(c * CHUNK, CHUNK), CHUNK)
        s = lax.dot_general(keys[rows, :], q, NT, preferred_element_type=F32)
        return s * scale

    def largest(c, top):
        return jnp.maximum(top, jnp.max(scores(c), axis=0, keepdims=True))

    top = lax.fori_loop(0, chunks, largest, jnp.full((1, LANES), -jnp.inf, F32))
    high, low = split_pair(top)
    shift = high + low

    def add(c, acc):
        rows = pl.ds(pl.multiple_of(c * CHUNK, CHUNK), CHUNK)
        p = jnp.exp2(scores(c) - shift).astype(BF16)
        return acc + jnp.dot(values_t[h, :, rows], p, preferred_element_type=F32)

    acc = lax.fori_loop(0, chunks, add, jnp.zeros((AUG, LANES), F32))
    return acc, high, low


def with_stats(acc, total, high, low):
    total_high, total_low = split_pair(total)
    row = lax.broadcasted_iota(jnp.int32, (AUG - HS, acc.shape[1]), 0)
    stats = jnp.where(row == 0, total_high, 0.0)
    stats = jnp.where(row == 1, total_low, stats)
    stats = jnp.where(row == 2, high, stats)
    stats = jnp.where(row == 3, low, stats)
    return jnp.concatenate([acc[:HS], stats], axis=0).astype(BF16)


def attend_chunk(qbuf, keys, values_t, sbuf, pbuf, out):
    blocks = qbuf.shape[0] // LANES

    def query(j, h):
        start = j * LANES if isinstance(j, int) else pl.multiple_of(j * LANES, LANES)
        q = qbuf[pl.ds(start, LANES), :]
        lane = lax.broadcasted_iota(jnp.int32, q.shape, 1)
        return jnp.where((lane < HS) == (h == 0), q, jnp.zeros_like(q))

    def emit_at(j, h, acc, high, low):
        out[j, h] = with_stats(acc, acc[HS : HS + 1], high, low)

    queries = [(h, query(j, h)) for j in range(blocks) for h in range(2)]
    above = attend_units(
        queries, keys, values_t, sbuf, pbuf, lambda u, *r: emit_at(u // 2, u % 2, *r)
    )

    @pl.when(jnp.logical_not(above <= SAFE))
    def _():
        def again(j, carry):
            for h in range(2):
                emit_at(j, h, *attend_exact(h, query(j, h), keys, values_t))
            return carry

        lax.fori_loop(0, blocks, again, 0)


def norm_rows(lbuf, row, xbuf):
    rows, width = lbuf.shape[1], lbuf.shape[2]
    for z in range(lbuf.shape[0]):
        part = pl.ds(z * rows, rows)
        x = lbuf[z].astype(F32)
        off = x - x[:, 0:1]
        mean = jnp.sum(off, axis=-1, keepdims=True) * (1.0 / width)
        spread = jnp.sum(off * off, axis=-1, keepdims=True) * (1.0 / width) - mean * mean
        factor = lax.rsqrt(jnp.maximum(spread, 0.0) + 1e-05)
        xbuf[part, :] = ((off - mean) * factor * row).astype(BF16)


def project_query(xbuf, wq, qbuf):
    qbuf[...] = lax.dot_general(xbuf[...], wq[...], NT, preferred_element_type=F32).astype(BF16)


def encode_kernel(
    where, points, latents, gain_in, gain_lat, wk_in, wv_in, wq_in,
    out0, out1, out2, keys_out, values_out,
    pts, lbuf, gbuf, hbuf, wk, wv, wq, keys, values_t, ybuf, xbuf, qbuf, sbuf, pbuf, sems,
):
    outs = (out0, out1, out2)
    pieces = [pl.ds(i * PIECE, PIECE) for i in range(pts.shape[0] // PIECE)]
    first = fetch(
        [(points.at[pieces[0], :], pts.at[pieces[0], :]), (gain_in, gbuf), (wk_in, wk), (wv_in, wv)]
        + [(points.at[rows, :], pts.at[rows, :]) for rows in pieces[1:]],
        sems,
    )
    later = fetch(
        [(gain_lat, hbuf), (wq_in, wq)]
        + [(latents.at[:, lax.rem(where[0] + k, NX)], lbuf.at[i]) for i, k in enumerate(FOREIGN)],
        sems.at[pl.ds(len(first), len(outs) + 2)],
    )
    back = fetch([(keys, keys_out), (values_t, values_out)], sems.at[pl.ds(0, 2)])
    for copy in first:
        copy.start()

    def ready(i):
        if i == 0:
            for copy in first[:4]:
                copy.wait()
            for copy in later:
                copy.start()
        else:
            first[3 + i].wait()

    project_points(pts, gbuf, wk, wv, keys, values_t, ybuf, ready)
    for copy in back:
        copy.start()
    later[0].wait()
    later[1].wait()
    row = gain_row(hbuf)
    for i, out in enumerate(outs):
        later[2 + i].wait()
        norm_rows(lbuf.at[i], row, xbuf)
        project_query(xbuf, wq, qbuf)
        attend_chunk(qbuf, keys, values_t, sbuf, pbuf, out)
    for copy in back:
        copy.wait()


def own_kernel(
    where, latents, gain, wq_in, keys_in, values_in, out,
    lbuf, gbuf, wq, keys, values_t, xbuf, qbuf, sbuf, pbuf, sems,
):
    copies = fetch(
        [(latents.at[:, where[0]], lbuf), (gain, gbuf), (wq_in, wq), (keys_in, keys), (values_in, values_t)],
        sems,
    )
    for copy in copies:
        copy.start()
    copies[0].wait()
    copies[1].wait()
    norm_rows(lbuf, gain_row(gbuf), xbuf)
    copies[2].wait()
    project_query(xbuf, wq, qbuf)
    copies[3].wait()
    copies[4].wait()
    attend_chunk(qbuf, keys, values_t, sbuf, pbuf, out)


def anywhere():
    return pl.BlockSpec(memory_space=pl.ANY)


def whole():
    return pl.BlockSpec(memory_space=pltpu.VMEM)


def anywhere():
    return pl.BlockSpec(memory_space=pl.ANY)


def attend_scratch(n):
    return [
        pltpu.VMEM((2, CHUNK, LANES), F32),
        pltpu.VMEM((2, n, LANES), BF16),
    ]


def encode_call(where, points, latents, gain_in, gain_lat, wk, wv, wq):
    n, width = points.shape
    nz, nx, rows, depth = latents.shape
    part = jax.ShapeDtypeStruct((nz * rows // LANES, 2, AUG, LANES), BF16)
    keys = jax.ShapeDtypeStruct((n, 2 * HS), BF16)
    values_t = jax.ShapeDtypeStruct((2, AUG, n), BF16)
    return pl.pallas_call(
        encode_kernel,
        out_shape=(part, part, part, keys, values_t),
        in_specs=[pl.BlockSpec(memory_space=pltpu.SMEM)] + [anywhere()] * 7,
        out_specs=(whole(), whole(), whole(), anywhere(), anywhere()),
        scratch_shapes=[
            pltpu.VMEM(points.shape, BF16),
            pltpu.VMEM((nx - 1, nz, rows, depth), BF16),
            pltpu.VMEM(gain_in.shape, F32),
            pltpu.VMEM(gain_lat.shape, F32),
            pltpu.VMEM(wk.shape, BF16),
            pltpu.VMEM(wv.shape, BF16),
            pltpu.VMEM(wq.shape, BF16),
            pltpu.VMEM(keys.shape, BF16),
            pltpu.VMEM(values_t.shape, BF16),
            pltpu.VMEM(points.shape, BF16),
            pltpu.VMEM((nz * rows, depth), BF16),
            pltpu.VMEM((nz * rows, 2 * HS), BF16),
        ]
        + attend_scratch(n)
        + [pltpu.SemaphoreType.DMA((n // PIECE + 8,))],
        compiler_params=pltpu.CompilerParams(vmem_limit_bytes=VMEM_WIDE),
        cost_estimate=pl.CostEstimate(
            flops=16 * 10**9, bytes_accessed=10**7, transcendentals=6 * 10**6
        ),
        name="encode",
    )(where, points, latents, gain_in, gain_lat, wk, wv, wq)


def own_call(where, latents, gain, wq, keys, values_t):
    nz, nx, rows, depth = latents.shape
    return pl.pallas_call(
        own_kernel,
        out_shape=jax.ShapeDtypeStruct((nz * rows // LANES, 2, AUG, LANES), BF16),
        in_specs=[pl.BlockSpec(memory_space=pltpu.SMEM)] + [anywhere()] * 5,
        out_specs=whole(),
        scratch_shapes=[
            pltpu.VMEM((nz, rows, depth), BF16),
            pltpu.VMEM(gain.shape, F32),
            pltpu.VMEM(wq.shape, BF16),
            pltpu.VMEM(keys.shape, BF16),
            pltpu.VMEM(values_t.shape, BF16),
            pltpu.VMEM((nz * rows, depth), BF16),
            pltpu.VMEM((nz * rows, 2 * HS), BF16),
        ]
        + attend_scratch(keys.shape[0])
        + [pltpu.SemaphoreType.DMA((5,))],
        compiler_params=pltpu.CompilerParams(vmem_limit_bytes=VMEM_WIDE),
        cost_estimate=pl.CostEstimate(
            flops=4 * 10**9, bytes_accessed=5 * 10**6, transcendentals=2 * 10**6
        ),
        name="own",
    )(where, latents, gain, wq, keys, values_t)


def merge(parts):
    shifts = [p[HS + 2 : HS + 3] + p[HS + 3 : HS + 4] for p in parts]
    high, low = split_pair(functools.reduce(jnp.maximum, shifts))
    top = high + low
    acc = functools.reduce(jnp.add, [p * jnp.exp2(s - top) for p, s in zip(parts, shifts)])
    return acc, acc[HS : HS + 1] + acc[HS + 1 : HS + 2], high, low


def combine_kernel(a, b, c, d, out):
    rows = out.shape[2] // 2
    per = LANES // rows
    for j in range(a.shape[0]):
        packed = []
        for h in range(2):
            acc, total, high, low = merge([r[j, h].astype(F32) for r in (a, b, c, d)])
            packed.append(with_stats(acc, total, high, low))
        for i in range(per):
            lanes = slice(i * rows, (i + 1) * rows)
            out[j * per + i] = jnp.concatenate([p[:, lanes] for p in packed], axis=1)


def finish(refs, rows):
    parts = [r[i].astype(F32) for r in refs for i in range(r.shape[0])]
    acc, total, _, _ = merge(parts)
    value = (acc[:HS] / total).T
    return jnp.concatenate([value[:rows], value[rows:]], axis=1).astype(BF16)


def finish_kernel(part, out):
    out[...] = finish([part], out.shape[0])


def near_kernel(a0, a1, a2, a3, w0, w1, w2, w3, out):
    total = None
    for a, w in ((a0, w0), (a1, w1), (a2, w2), (a3, w3)):
        term = jnp.dot(a[...], w[...], preferred_element_type=F32)
        total = term if total is None else total + term
    out[...] = total


def middle_kernel(latents, gain, own, other, wq, wk, wv, mid, q, kv):
    total = latents[...].astype(F32) + (own[...] + other[...])
    mid[...] = total
    x = normed(total, gain_row(gain))
    q[...] = lax.dot_general(x, wq[...], NT, preferred_element_type=F32).astype(BF16)
    k = lax.dot_general(x, wk[...], NT, preferred_element_type=F32).astype(BF16)
    v = lax.dot_general(x, wv[...], NT, preferred_element_type=F32).astype(BF16)
    both = jnp.concatenate([k, v], axis=1)
    for i in range(kv.shape[0]):
        kv[i] = both


def self_kernel(kv, q0, q1, q2, q3, out):
    scale = LOG2E * HS ** (-0.5)
    width = 2 * HS
    rows = q0.shape[0]
    keys = kv[:, 0:width]
    values_t = kv[:, width : 2 * width].astype(F32).T.astype(BF16)
    lane = lax.broadcasted_iota(jnp.int32, (rows, width), 1)
    first = lax.broadcasted_iota(jnp.int32, (HS, 2 * rows), 1) < rows
    for i, ref in enumerate((q0, q1, q2, q3)):
        q = ref[...]
        zero = jnp.zeros_like(q)
        both = jnp.concatenate([jnp.where(lane < HS, q, zero), jnp.where(lane < HS, zero, q)], axis=0)
        s = lax.dot_general(keys, both, NT, preferred_element_type=F32) * scale
        high, low = split_pair(jnp.max(s, axis=0, keepdims=True))
        p = jnp.exp2(s - (high + low))
        total = jnp.sum(p, axis=0, keepdims=True)
        n = jnp.dot(values_t, p.astype(BF16), preferred_element_type=F32)
        out[i] = with_stats(jnp.where(first, n[:HS], n[HS:]), total, high, low)


def output_kernel(p0, p1, p2, p3, w, out):
    count, rows, width = out.shape
    attn = finish([p0, p1, p2, p3], rows)
    terms = jnp.dot(attn, w[...], preferred_element_type=F32)
    for i in range(count):
        out[i] = terms[:, i * width : (i + 1) * width].astype(BF16)


def add_kernel(mid, terms, out):
    total = mid[...]
    for i in range(terms.shape[0]):
        total = total + terms[i].astype(F32)
    out[...] = total.astype(BF16)


def plain_call(kernel, name, out_shape, *args, flops=6 * 10**9):
    moved = sum(a.size * a.dtype.itemsize for a in args)
    spec = lambda a: pl.BlockSpec(memory_space=pltpu.SMEM) if a.dtype == jnp.int32 else whole()
    return pl.pallas_call(
        kernel,
        out_shape=out_shape,
        in_specs=[spec(a) for a in args],
        out_specs=jax.tree.map(lambda _: whole(), out_shape),
        compiler_params=pltpu.CompilerParams(vmem_limit_bytes=VMEM_LIMIT),
        cost_estimate=pl.CostEstimate(flops=flops, bytes_accessed=moved, transcendentals=0),
        name=name,
    )(*args)


def permute_x(v, k):
    return lax.ppermute(
        v, "seq", [(i, (i // NX) * NX + (i % NX + k) % NX) for i in range(NX * NZ)]
    )


def permute_y(v, k):
    return lax.ppermute(v, "head", [(i, (i + 2 * k) % (2 * NY)) for i in range(2 * NY)])


def swap_cores(v):
    return lax.ppermute(v, "head", [(i, i ^ 1) for i in range(2 * NY)])


def gather_y(v):
    return [v] + [permute_y(v, k) for k in SHIFTS]


def body(
    points,
    latents,
    gain_in,
    gain_lat,
    gain_self,
    cross_query,
    cross_key,
    cross_value,
    cross_out,
    self_query,
    latent_key_weight,
    self_value,
    self_out,
):
    width = cross_query.shape[1]
    count, depth = latents.shape
    rows = count // (NX * NZ)
    seq = lax.axis_index("seq").astype(jnp.int32)
    head = lax.axis_index("head").astype(jnp.int32)
    part_shape = jax.ShapeDtypeStruct((NZ, AUG, 2 * rows), BF16)
    gains = [g.reshape(-1, 128) for g in (gain_in, gain_lat, gain_self)]

    out_near = [cross_out] + [permute_y(cross_out, k) for k in SHIFTS[:2]]
    latents_4d = latents.reshape(NZ, NX, rows, depth)
    x = (seq % NX).reshape(1)
    *sent, keys, values_t = encode_call(
        x, points, latents_4d, gains[0], gains[1], cross_key.T, cross_value.T, cross_query.T
    )
    parts = [permute_x(v, k) for v, k in zip(sent, FOREIGN)]
    part = own_call(x, latents_4d, gains[1], cross_query.T, keys, values_t)
    part = plain_call(combine_kernel, "combine", part_shape, part, *parts)
    part, last = lax.optimization_barrier((part, cross_out))
    out_near.append(permute_y(last, SHIFTS[2]))
    lat_rows = lax.dynamic_slice_in_dim(latents, seq * rows, rows, 0)
    part = lax.all_to_all(part, "seq", 0, 0, axis_index_groups=Z_GROUPS)
    part, out_near, lat_rows = lax.optimization_barrier((part, out_near, lat_rows))
    block = jax.ShapeDtypeStruct((rows, width), BF16)
    cross_attn = plain_call(finish_kernel, "finish", block, part)
    own = plain_call(
        near_kernel, "near", jax.ShapeDtypeStruct((rows, depth), F32), *gather_y(cross_attn), *out_near
    )
    mid, squery, kv = plain_call(
        middle_kernel, "middle",
        (
            jax.ShapeDtypeStruct((rows, depth), F32),
            block,
            jax.ShapeDtypeStruct((NZ, rows, 2 * width), BF16),
        ),
        lat_rows, gains[2], own, swap_cores(own),
        self_query.T, latent_key_weight.T, self_value.T,
    )
    kv = lax.all_to_all(kv, "seq", 0, 0, axis_index_groups=Z_GROUPS)
    squeries = [squery] + [permute_x(squery, k) for k in SHIFTS]
    mid_cols = lax.dynamic_slice_in_dim(mid, head * width, width, 1)
    kv, mid_cols = lax.optimization_barrier((kv, mid_cols))
    part = plain_call(
        self_kernel, "self_part", jax.ShapeDtypeStruct((NX, AUG, 2 * rows), BF16),
        kv.reshape(NZ * rows, 2 * width), *squeries,
    )
    back = [part[0:1]] + [permute_x(part[i + 1 : i + 2], -k) for i, k in enumerate(SHIFTS)]
    terms = plain_call(
        output_kernel, "output", jax.ShapeDtypeStruct((2 * NY, rows, width), BF16), *back, self_out
    )
    terms = lax.all_to_all(terms, "head", 0, 0)
    return plain_call(add_kernel, "add", block, mid_cols, terms)


def solution(mesh):
    in_specs = (
        P("seq", None),
        P(),
        P(),
        P(),
        P(),
        P(None, "head"),
        P(None, "head"),
        P(None, "head"),
        P("head", None),
        P(None, "head"),
        P(None, "head"),
        P(None, "head"),
        P("head", None),
    )
    out_specs = P("seq", "head")
    return jax.shard_map(body, mesh=mesh, in_specs=in_specs, out_specs=out_specs, check_vma=False)
```

```python
import functools
import jax
import jax.numpy as jnp
from jax import lax
from jax.experimental import pallas as pl
from jax.experimental.pallas import tpu as pltpu
from jax.sharding import PartitionSpec as P

NX = 4
NY = 4
NZ = 8
Z_GROUPS = [[z * NX + x for z in range(NZ)] for x in range(NX)]
SHIFTS = (1, NX - 1, 2)
FOREIGN = (2, 1, NX - 1)

HS = 96
AUG = 112
LANES = 256
CHUNK = 256
PIECE = 512
LOG2E = 1.4426950408889634
SAFE = 2.0**64
F32 = jnp.float32
BF16 = jnp.bfloat16
NT = (((1,), (1,)), ((), ()))
VMEM_LIMIT = 20 * 1024 * 1024
VMEM_WIDE = 58 * 1024 * 1024


def normed(values, gain):
    values = values.astype(F32)
    center = values - jnp.mean(values, axis=-1, keepdims=True)
    spread = jnp.mean(center * center, axis=-1, keepdims=True)
    return (center * lax.rsqrt(spread + 1e-05) * gain).astype(BF16)


def gain_row(gain):
    return jnp.concatenate([gain[i : i + 1, :] for i in range(gain.shape[0])], axis=1)


def split_pair(value):
    high = value.astype(BF16).astype(F32)
    return high, (value - high).astype(BF16).astype(F32)


def fetch(pairs, sems):
    return [pltpu.make_async_copy(src, dst, sems.at[i]) for i, (src, dst) in enumerate(pairs)]


def project_points(pbuf, gain, wk, wv, keys, values_t, xbuf, ready):
    for i in range(pbuf.shape[0] // PIECE):
        ready(i)
        row = gain_row(gain)
        for j in range(i * PIECE, (i + 1) * PIECE, 64):
            xbuf[j : j + 64, :] = normed(pbuf[j : j + 64, :], row)
    x = xbuf[...]
    keys[...] = lax.dot_general(x, wk[...], NT, preferred_element_type=F32).astype(BF16)
    vt = lax.dot_general(wv[...], x, NT, preferred_element_type=F32).astype(BF16)
    for h in range(2):
        values_t[h, 0:HS, :] = vt[h * HS : (h + 1) * HS]
    one = lax.broadcasted_iota(jnp.int32, (AUG - HS, pbuf.shape[0]), 0) == 0
    for h in range(2):
        values_t[h, HS:AUG, :] = one.astype(BF16)


def attend_units(queries, keys, values_t, sbuf, pbuf, emit):
    count = keys.shape[0]
    scale = LOG2E * HS ** (-0.5)
    chunks = count // CHUNK

    def score(u, c):
        rows = pl.ds(c * CHUNK, CHUNK)
        return lax.dot_general(keys[rows, :], queries[u][1], NT, preferred_element_type=F32)

    def first(u):
        s = score(u, 0)
        sbuf[u % 2] = s
        return split_pair(jnp.max(s, axis=0, keepdims=True) * scale)

    largest = jnp.zeros((1, LANES), F32)
    state = first(0)
    for u, (h, q) in enumerate(queries):
        high, low = state
        shift = high + low
        for c in range(chunks):
            s = sbuf[u % 2] if c == 0 else score(u, c)
            pbuf[u % 2, c * CHUNK : (c + 1) * CHUNK, :] = jnp.exp2(s * scale - shift).astype(BF16)
        acc = jnp.dot(values_t[h], pbuf[u % 2], preferred_element_type=F32)
        if u + 1 < len(queries):
            state = first(u + 1)
        emit(u, acc, high, low)
        largest = jnp.maximum(largest, acc[HS : HS + 1])
    return jnp.max(largest)


def attend_exact(h, q, keys, values_t):
    scale = LOG2E * HS ** (-0.5)
    chunks = keys.shape[0] // CHUNK

    def scores(c):
        rows = pl.ds(pl.multiple_of(c * CHUNK, CHUNK), CHUNK)
        s = lax.dot_general(keys[rows, :], q, NT, preferred_element_type=F32)
        return s * scale

    def largest(c, top):
        return jnp.maximum(top, jnp.max(scores(c), axis=0, keepdims=True))

    top = lax.fori_loop(0, chunks, largest, jnp.full((1, LANES), -jnp.inf, F32))
    high, low = split_pair(top)
    shift = high + low

    def add(c, acc):
        rows = pl.ds(pl.multiple_of(c * CHUNK, CHUNK), CHUNK)
        p = jnp.exp2(scores(c) - shift).astype(BF16)
        return acc + jnp.dot(values_t[h, :, rows], p, preferred_element_type=F32)

    acc = lax.fori_loop(0, chunks, add, jnp.zeros((AUG, LANES), F32))
    return acc, high, low


def with_stats(acc, total, high, low):
    total_high, total_low = split_pair(total)
    row = lax.broadcasted_iota(jnp.int32, (AUG - HS, acc.shape[1]), 0)
    stats = jnp.where(row == 0, total_high, 0.0)
    stats = jnp.where(row == 1, total_low, stats)
    stats = jnp.where(row == 2, high, stats)
    stats = jnp.where(row == 3, low, stats)
    return jnp.concatenate([acc[:HS], stats], axis=0).astype(BF16)


def attend_chunk(qbuf, keys, values_t, sbuf, pbuf, out):
    blocks = qbuf.shape[0] // LANES

    def query(j, h):
        start = j * LANES if isinstance(j, int) else pl.multiple_of(j * LANES, LANES)
        q = qbuf[pl.ds(start, LANES), :]
        lane = lax.broadcasted_iota(jnp.int32, q.shape, 1)
        return jnp.where((lane < HS) == (h == 0), q, jnp.zeros_like(q))

    def emit_at(j, h, acc, high, low):
        out[j, h] = with_stats(acc, acc[HS : HS + 1], high, low)

    queries = [(h, query(j, h)) for j in range(blocks) for h in range(2)]
    above = attend_units(
        queries, keys, values_t, sbuf, pbuf, lambda u, *r: emit_at(u // 2, u % 2, *r)
    )

    @pl.when(jnp.logical_not(above <= SAFE))
    def _():
        def again(j, carry):
            for h in range(2):
                emit_at(j, h, *attend_exact(h, query(j, h), keys, values_t))
            return carry

        lax.fori_loop(0, blocks, again, 0)


def norm_rows(lbuf, row, xbuf):
    rows, width = lbuf.shape[1], lbuf.shape[2]
    for z in range(lbuf.shape[0]):
        part = pl.ds(z * rows, rows)
        x = lbuf[z].astype(F32)
        off = x - x[:, 0:1]
        mean = jnp.sum(off, axis=-1, keepdims=True) * (1.0 / width)
        spread = jnp.sum(off * off, axis=-1, keepdims=True) * (1.0 / width) - mean * mean
        factor = lax.rsqrt(jnp.maximum(spread, 0.0) + 1e-05)
        xbuf[part, :] = ((off - mean) * factor * row).astype(BF16)


def project_query(xbuf, wq, qbuf):
    qbuf[...] = lax.dot_general(xbuf[...], wq[...], NT, preferred_element_type=F32).astype(BF16)


def encode_kernel(
    where, points, latents, gain_in, gain_lat, wk_in, wv_in, wq_in,
    out0, out1, out2, keys_out, values_out,
    pts, lbuf, gbuf, hbuf, wk, wv, wq, keys, values_t, ybuf, xbuf, qbuf, sbuf, pbuf, sems,
):
    outs = (out0, out1, out2)
    pieces = [pl.ds(i * PIECE, PIECE) for i in range(pts.shape[0] // PIECE)]
    first = fetch(
        [(points.at[pieces[0], :], pts.at[pieces[0], :]), (gain_in, gbuf), (wk_in, wk), (wv_in, wv)]
        + [(points.at[rows, :], pts.at[rows, :]) for rows in pieces[1:]],
        sems,
    )
    later = fetch(
        [(gain_lat, hbuf), (wq_in, wq)]
        + [(latents.at[:, lax.rem(where[0] + k, NX)], lbuf.at[i]) for i, k in enumerate(FOREIGN)],
        sems.at[pl.ds(len(first), len(outs) + 2)],
    )
    back = fetch([(keys, keys_out), (values_t, values_out)], sems.at[pl.ds(0, 2)])
    for copy in first:
        copy.start()

    def ready(i):
        if i == 0:
            for copy in first[:4]:
                copy.wait()
            for copy in later:
                copy.start()
        else:
            first[3 + i].wait()

    project_points(pts, gbuf, wk, wv, keys, values_t, ybuf, ready)
    for copy in back:
        copy.start()
    later[0].wait()
    later[1].wait()
    row = gain_row(hbuf)
    for i, out in enumerate(outs):
        later[2 + i].wait()
        norm_rows(lbuf.at[i], row, xbuf)
        project_query(xbuf, wq, qbuf)
        attend_chunk(qbuf, keys, values_t, sbuf, pbuf, out)
    for copy in back:
        copy.wait()


def own_kernel(
    where, latents, gain, wq_in, keys_in, values_in, out,
    lbuf, gbuf, wq, keys, values_t, xbuf, qbuf, sbuf, pbuf, sems,
):
    copies = fetch(
        [(latents.at[:, where[0]], lbuf), (gain, gbuf), (wq_in, wq), (keys_in, keys), (values_in, values_t)],
        sems,
    )
    for copy in copies:
        copy.start()
    copies[0].wait()
    copies[1].wait()
    norm_rows(lbuf, gain_row(gbuf), xbuf)
    copies[2].wait()
    project_query(xbuf, wq, qbuf)
    copies[3].wait()
    copies[4].wait()
    attend_chunk(qbuf, keys, values_t, sbuf, pbuf, out)


def anywhere():
    return pl.BlockSpec(memory_space=pl.ANY)


def whole():
    return pl.BlockSpec(memory_space=pltpu.VMEM)


def anywhere():
    return pl.BlockSpec(memory_space=pl.ANY)


def attend_scratch(n):
    return [
        pltpu.VMEM((2, CHUNK, LANES), F32),
        pltpu.VMEM((2, n, LANES), BF16),
    ]


def encode_call(where, points, latents, gain_in, gain_lat, wk, wv, wq):
    n, width = points.shape
    nz, nx, rows, depth = latents.shape
    part = jax.ShapeDtypeStruct((nz * rows // LANES, 2, AUG, LANES), BF16)
    keys = jax.ShapeDtypeStruct((n, 2 * HS), BF16)
    values_t = jax.ShapeDtypeStruct((2, AUG, n), BF16)
    return pl.pallas_call(
        encode_kernel,
        out_shape=(part, part, part, keys, values_t),
        in_specs=[pl.BlockSpec(memory_space=pltpu.SMEM)] + [anywhere()] * 7,
        out_specs=(whole(), whole(), whole(), anywhere(), anywhere()),
        scratch_shapes=[
            pltpu.VMEM(points.shape, BF16),
            pltpu.VMEM((nx - 1, nz, rows, depth), BF16),
            pltpu.VMEM(gain_in.shape, F32),
            pltpu.VMEM(gain_lat.shape, F32),
            pltpu.VMEM(wk.shape, BF16),
            pltpu.VMEM(wv.shape, BF16),
            pltpu.VMEM(wq.shape, BF16),
            pltpu.VMEM(keys.shape, BF16),
            pltpu.VMEM(values_t.shape, BF16),
            pltpu.VMEM(points.shape, BF16),
            pltpu.VMEM((nz * rows, depth), BF16),
            pltpu.VMEM((nz * rows, 2 * HS), BF16),
        ]
        + attend_scratch(n)
        + [pltpu.SemaphoreType.DMA((n // PIECE + 8,))],
        compiler_params=pltpu.CompilerParams(vmem_limit_bytes=VMEM_WIDE),
        cost_estimate=pl.CostEstimate(
            flops=16 * 10**9, bytes_accessed=10**7, transcendentals=6 * 10**6
        ),
        name="encode",
    )(where, points, latents, gain_in, gain_lat, wk, wv, wq)


def own_call(where, latents, gain, wq, keys, values_t):
    nz, nx, rows, depth = latents.shape
    return pl.pallas_call(
        own_kernel,
        out_shape=jax.ShapeDtypeStruct((nz * rows // LANES, 2, AUG, LANES), BF16),
        in_specs=[pl.BlockSpec(memory_space=pltpu.SMEM)] + [anywhere()] * 5,
        out_specs=whole(),
        scratch_shapes=[
            pltpu.VMEM((nz, rows, depth), BF16),
            pltpu.VMEM(gain.shape, F32),
            pltpu.VMEM(wq.shape, BF16),
            pltpu.VMEM(keys.shape, BF16),
            pltpu.VMEM(values_t.shape, BF16),
            pltpu.VMEM((nz * rows, depth), BF16),
            pltpu.VMEM((nz * rows, 2 * HS), BF16),
        ]
        + attend_scratch(keys.shape[0])
        + [pltpu.SemaphoreType.DMA((5,))],
        compiler_params=pltpu.CompilerParams(vmem_limit_bytes=VMEM_WIDE),
        cost_estimate=pl.CostEstimate(
            flops=4 * 10**9, bytes_accessed=5 * 10**6, transcendentals=2 * 10**6
        ),
        name="own",
    )(where, latents, gain, wq, keys, values_t)


def merge(parts):
    shifts = [p[HS + 2 : HS + 3] + p[HS + 3 : HS + 4] for p in parts]
    high, low = split_pair(functools.reduce(jnp.maximum, shifts))
    top = high + low
    acc = functools.reduce(jnp.add, [p * jnp.exp2(s - top) for p, s in zip(parts, shifts)])
    return acc, acc[HS : HS + 1] + acc[HS + 1 : HS + 2], high, low


def combine_kernel(a, b, c, d, out):
    rows = out.shape[2] // 2
    per = LANES // rows
    for j in range(a.shape[0]):
        packed = []
        for h in range(2):
            acc, total, high, low = merge([r[j, h].astype(F32) for r in (a, b, c, d)])
            packed.append(with_stats(acc, total, high, low))
        for i in range(per):
            lanes = slice(i * rows, (i + 1) * rows)
            out[j * per + i] = jnp.concatenate([p[:, lanes] for p in packed], axis=1)


def finish(refs, rows):
    parts = [r[i].astype(F32) for r in refs for i in range(r.shape[0])]
    acc, total, _, _ = merge(parts)
    value = (acc[:HS] / total).T
    return jnp.concatenate([value[:rows], value[rows:]], axis=1).astype(BF16)


def finish_kernel(part, out):
    out[...] = finish([part], out.shape[0])


def near_kernel(a0, a1, a2, a3, w0, w1, w2, w3, out):
    total = None
    for a, w in ((a0, w0), (a1, w1), (a2, w2), (a3, w3)):
        term = jnp.dot(a[...], w[...], preferred_element_type=F32)
        total = term if total is None else total + term
    out[...] = total


def middle_kernel(latents, gain, own, other, wq, wk, wv, mid, q, kv):
    total = latents[...].astype(F32) + (own[...] + other[...])
    mid[...] = total
    x = normed(total, gain_row(gain))
    q[...] = lax.dot_general(x, wq[...], NT, preferred_element_type=F32).astype(BF16)
    k = lax.dot_general(x, wk[...], NT, preferred_element_type=F32).astype(BF16)
    v = lax.dot_general(x, wv[...], NT, preferred_element_type=F32).astype(BF16)
    both = jnp.concatenate([k, v], axis=1)
    for i in range(kv.shape[0]):
        kv[i] = both


def self_kernel(kv, q0, q1, q2, q3, out):
    scale = LOG2E * HS ** (-0.5)
    width = 2 * HS
    rows = q0.shape[0]
    keys = kv[:, 0:width]
    values_t = kv[:, width : 2 * width].astype(F32).T.astype(BF16)
    lane = lax.broadcasted_iota(jnp.int32, (rows, width), 1)
    first = lax.broadcasted_iota(jnp.int32, (HS, 2 * rows), 1) < rows
    for i, ref in enumerate((q0, q1, q2, q3)):
        q = ref[...]
        zero = jnp.zeros_like(q)
        both = jnp.concatenate([jnp.where(lane < HS, q, zero), jnp.where(lane < HS, zero, q)], axis=0)
        s = lax.dot_general(keys, both, NT, preferred_element_type=F32) * scale
        high, low = split_pair(jnp.max(s, axis=0, keepdims=True))
        p = jnp.exp2(s - (high + low))
        total = jnp.sum(p, axis=0, keepdims=True)
        n = jnp.dot(values_t, p.astype(BF16), preferred_element_type=F32)
        out[i] = with_stats(jnp.where(first, n[:HS], n[HS:]), total, high, low)


def output_kernel(p0, p1, p2, p3, w, out):
    count, rows, width = out.shape
    attn = finish([p0, p1, p2, p3], rows)
    terms = jnp.dot(attn, w[...], preferred_element_type=F32)
    for i in range(count):
        out[i] = terms[:, i * width : (i + 1) * width].astype(BF16)


def add_kernel(mid, terms, out):
    total = mid[...]
    for i in range(terms.shape[0]):
        total = total + terms[i].astype(F32)
    out[...] = total.astype(BF16)


def plain_call(kernel, name, out_shape, *args, flops=6 * 10**9):
    moved = sum(a.size * a.dtype.itemsize for a in args)
    spec = lambda a: pl.BlockSpec(memory_space=pltpu.SMEM) if a.dtype == jnp.int32 else whole()
    return pl.pallas_call(
        kernel,
        out_shape=out_shape,
        in_specs=[spec(a) for a in args],
        out_specs=jax.tree.map(lambda _: whole(), out_shape),
        compiler_params=pltpu.CompilerParams(vmem_limit_bytes=VMEM_LIMIT),
        cost_estimate=pl.CostEstimate(flops=flops, bytes_accessed=moved, transcendentals=0),
        name=name,
    )(*args)


def permute_x(v, k):
    return lax.ppermute(
        v, "seq", [(i, (i // NX) * NX + (i % NX + k) % NX) for i in range(NX * NZ)]
    )


def permute_y(v, k):
    return lax.ppermute(v, "head", [(i, (i + 2 * k) % (2 * NY)) for i in range(2 * NY)])


def swap_cores(v):
    return lax.ppermute(v, "head", [(i, i ^ 1) for i in range(2 * NY)])


def gather_y(v):
    got = {k: permute_y(v, k) for k in FOREIGN}
    return [v] + [got[k] for k in SHIFTS]


def body(
    points,
    latents,
    gain_in,
    gain_lat,
    gain_self,
    cross_query,
    cross_key,
    cross_value,
    cross_out,
    self_query,
    latent_key_weight,
    self_value,
    self_out,
):
    width = cross_query.shape[1]
    count, depth = latents.shape
    rows = count // (NX * NZ)
    seq = lax.axis_index("seq").astype(jnp.int32)
    head = lax.axis_index("head").astype(jnp.int32)
    part_shape = jax.ShapeDtypeStruct((NZ, AUG, 2 * rows), BF16)
    gains = [g.reshape(-1, 128) for g in (gain_in, gain_lat, gain_self)]

    out_near = [cross_out] + [permute_y(cross_out, k) for k in SHIFTS[:2]]
    latents_4d = latents.reshape(NZ, NX, rows, depth)
    x = (seq % NX).reshape(1)
    *sent, keys, values_t = encode_call(
        x, points, latents_4d, gains[0], gains[1], cross_key.T, cross_value.T, cross_query.T
    )
    parts = [permute_x(v, k) for v, k in zip(sent, FOREIGN)]
    part = own_call(x, latents_4d, gains[1], cross_query.T, keys, values_t)
    part = plain_call(combine_kernel, "combine", part_shape, part, *parts)
    part, last = lax.optimization_barrier((part, cross_out))
    out_near.append(permute_y(last, SHIFTS[2]))
    lat_rows = lax.dynamic_slice_in_dim(latents, seq * rows, rows, 0)
    part = lax.all_to_all(part, "seq", 0, 0, axis_index_groups=Z_GROUPS)
    part, out_near, lat_rows = lax.optimization_barrier((part, out_near, lat_rows))
    block = jax.ShapeDtypeStruct((rows, width), BF16)
    cross_attn = plain_call(finish_kernel, "finish", block, part)
    own = plain_call(
        near_kernel, "near", jax.ShapeDtypeStruct((rows, depth), F32), *gather_y(cross_attn), *out_near
    )
    mid, squery, kv = plain_call(
        middle_kernel, "middle",
        (
            jax.ShapeDtypeStruct((rows, depth), F32),
            block,
            jax.ShapeDtypeStruct((NZ, rows, 2 * width), BF16),
        ),
        lat_rows, gains[2], own, swap_cores(own),
        self_query.T, latent_key_weight.T, self_value.T,
    )
    kv = lax.all_to_all(kv, "seq", 0, 0, axis_index_groups=Z_GROUPS)
    squeries = [squery] + [permute_x(squery, k) for k in SHIFTS]
    mid_cols = lax.dynamic_slice_in_dim(mid, head * width, width, 1)
    kv, mid_cols = lax.optimization_barrier((kv, mid_cols))
    part = plain_call(
        self_kernel, "self_part", jax.ShapeDtypeStruct((NX, AUG, 2 * rows), BF16),
        kv.reshape(NZ * rows, 2 * width), *squeries,
    )
    back = [part[0:1]] + [permute_x(part[i + 1 : i + 2], -k) for i, k in enumerate(SHIFTS)]
    terms = plain_call(
        output_kernel, "output", jax.ShapeDtypeStruct((2 * NY, rows, width), BF16), *back, self_out
    )
    terms = lax.all_to_all(terms, "head", 0, 0)
    return plain_call(add_kernel, "add", block, mid_cols, terms)


def solution(mesh):
    in_specs = (
        P("seq", None),
        P(),
        P(),
        P(),
        P(),
        P(None, "head"),
        P(None, "head"),
        P(None, "head"),
        P("head", None),
        P(None, "head"),
        P(None, "head"),
        P(None, "head"),
        P("head", None),
    )
    out_specs = P("seq", "head")
    return jax.shard_map(body, mesh=mesh, in_specs=in_specs, out_specs=out_specs, check_vma=False)
```

```python
import functools
import jax
import jax.numpy as jnp
from jax import lax
from jax.experimental import pallas as pl
from jax.experimental.pallas import tpu as pltpu
from jax.sharding import PartitionSpec as P

NX = 4
NY = 4
NZ = 8
Z_GROUPS = [[z * NX + x for z in range(NZ)] for x in range(NX)]
SHIFTS = (1, NX - 1, 2)
FOREIGN = (2, 1, NX - 1)

HS = 96
AUG = 112
LANES = 256
CHUNK = 256
PIECE = 512
LOG2E = 1.4426950408889634
SAFE = 2.0**64
F32 = jnp.float32
BF16 = jnp.bfloat16
NT = (((1,), (1,)), ((), ()))
VMEM_LIMIT = 20 * 1024 * 1024
VMEM_WIDE = 58 * 1024 * 1024


def normed(values, gain):
    values = values.astype(F32)
    center = values - jnp.mean(values, axis=-1, keepdims=True)
    spread = jnp.mean(center * center, axis=-1, keepdims=True)
    return (center * lax.rsqrt(spread + 1e-05) * gain).astype(BF16)


def gain_row(gain):
    return jnp.concatenate([gain[i : i + 1, :] for i in range(gain.shape[0])], axis=1)


def split_pair(value):
    high = value.astype(BF16).astype(F32)
    return high, (value - high).astype(BF16).astype(F32)


def fetch(pairs, sems):
    return [pltpu.make_async_copy(src, dst, sems.at[i]) for i, (src, dst) in enumerate(pairs)]


def project_points(pbuf, gain, wk, wv, keys, values_t, xbuf, ready):
    for i in range(pbuf.shape[0] // PIECE):
        ready(i)
        row = gain_row(gain)
        for j in range(i * PIECE, (i + 1) * PIECE, 64):
            xbuf[j : j + 64, :] = normed(pbuf[j : j + 64, :], row)
    x = xbuf[...]
    keys[...] = lax.dot_general(x, wk[...], NT, preferred_element_type=F32).astype(BF16)
    vt = lax.dot_general(wv[...], x, NT, preferred_element_type=F32).astype(BF16)
    for h in range(2):
        values_t[h, 0:HS, :] = vt[h * HS : (h + 1) * HS]
    one = lax.broadcasted_iota(jnp.int32, (AUG - HS, pbuf.shape[0]), 0) == 0
    for h in range(2):
        values_t[h, HS:AUG, :] = one.astype(BF16)


def attend_units(queries, keys, values_t, sbuf, pbuf, emit):
    count = keys.shape[0]
    scale = LOG2E * HS ** (-0.5)
    chunks = count // CHUNK

    def score(u, c):
        rows = pl.ds(c * CHUNK, CHUNK)
        return lax.dot_general(keys[rows, :], queries[u][1], NT, preferred_element_type=F32)

    def first(u):
        s = score(u, 0)
        sbuf[u % 2] = s
        return split_pair(jnp.max(s, axis=0, keepdims=True) * scale)

    largest = jnp.zeros((1, LANES), F32)
    state = first(0)
    for u, (h, q) in enumerate(queries):
        high, low = state
        shift = high + low
        for c in range(chunks):
            s = sbuf[u % 2] if c == 0 else score(u, c)
            pbuf[u % 2, c * CHUNK : (c + 1) * CHUNK, :] = jnp.exp2(s * scale - shift).astype(BF16)
        acc = jnp.dot(values_t[h], pbuf[u % 2], preferred_element_type=F32)
        if u + 1 < len(queries):
            state = first(u + 1)
        emit(u, acc, high, low)
        largest = jnp.maximum(largest, acc[HS : HS + 1])
    return jnp.max(largest)


def attend_exact(h, q, keys, values_t):
    scale = LOG2E * HS ** (-0.5)
    chunks = keys.shape[0] // CHUNK

    def scores(c):
        rows = pl.ds(pl.multiple_of(c * CHUNK, CHUNK), CHUNK)
        s = lax.dot_general(keys[rows, :], q, NT, preferred_element_type=F32)
        return s * scale

    def largest(c, top):
        return jnp.maximum(top, jnp.max(scores(c), axis=0, keepdims=True))

    top = lax.fori_loop(0, chunks, largest, jnp.full((1, LANES), -jnp.inf, F32))
    high, low = split_pair(top)
    shift = high + low

    def add(c, acc):
        rows = pl.ds(pl.multiple_of(c * CHUNK, CHUNK), CHUNK)
        p = jnp.exp2(scores(c) - shift).astype(BF16)
        return acc + jnp.dot(values_t[h, :, rows], p, preferred_element_type=F32)

    acc = lax.fori_loop(0, chunks, add, jnp.zeros((AUG, LANES), F32))
    return acc, high, low


def with_stats(acc, total, high, low):
    total_high, total_low = split_pair(total)
    row = lax.broadcasted_iota(jnp.int32, (AUG - HS, acc.shape[1]), 0)
    stats = jnp.where(row == 0, total_high, 0.0)
    stats = jnp.where(row == 1, total_low, stats)
    stats = jnp.where(row == 2, high, stats)
    stats = jnp.where(row == 3, low, stats)
    return jnp.concatenate([acc[:HS], stats], axis=0).astype(BF16)


def attend_chunk(qbuf, keys, values_t, sbuf, pbuf, out):
    blocks = qbuf.shape[0] // LANES

    def query(j, h):
        start = j * LANES if isinstance(j, int) else pl.multiple_of(j * LANES, LANES)
        q = qbuf[pl.ds(start, LANES), :]
        lane = lax.broadcasted_iota(jnp.int32, q.shape, 1)
        return jnp.where((lane < HS) == (h == 0), q, jnp.zeros_like(q))

    def emit_at(j, h, acc, high, low):
        out[j, h] = with_stats(acc, acc[HS : HS + 1], high, low)

    queries = [(h, query(j, h)) for j in range(blocks) for h in range(2)]
    above = attend_units(
        queries, keys, values_t, sbuf, pbuf, lambda u, *r: emit_at(u // 2, u % 2, *r)
    )

    @pl.when(jnp.logical_not(above <= SAFE))
    def _():
        def again(j, carry):
            for h in range(2):
                emit_at(j, h, *attend_exact(h, query(j, h), keys, values_t))
            return carry

        lax.fori_loop(0, blocks, again, 0)


def norm_rows(lbuf, row, xbuf):
    rows, width = lbuf.shape[1], lbuf.shape[2]
    for z in range(lbuf.shape[0]):
        part = pl.ds(z * rows, rows)
        x = lbuf[z].astype(F32)
        off = x - x[:, 0:1]
        mean = jnp.sum(off, axis=-1, keepdims=True) * (1.0 / width)
        spread = jnp.sum(off * off, axis=-1, keepdims=True) * (1.0 / width) - mean * mean
        factor = lax.rsqrt(jnp.maximum(spread, 0.0) + 1e-05)
        xbuf[part, :] = ((off - mean) * factor * row).astype(BF16)


def project_query(xbuf, wq, qbuf):
    qbuf[...] = lax.dot_general(xbuf[...], wq[...], NT, preferred_element_type=F32).astype(BF16)


def encode_kernel(
    where, points, latents, gain_in, gain_lat, wk_in, wv_in, wq_in,
    out0, out1, out2, keys_out, values_out,
    pts, lbuf, gbuf, hbuf, wk, wv, wq, keys, values_t, ybuf, xbuf, qbuf, sbuf, pbuf, sems,
):
    outs = (out0, out1, out2)
    pieces = [pl.ds(i * PIECE, PIECE) for i in range(pts.shape[0] // PIECE)]
    first = fetch(
        [(points.at[pieces[0], :], pts.at[pieces[0], :]), (gain_in, gbuf), (wk_in, wk), (wv_in, wv)]
        + [(points.at[rows, :], pts.at[rows, :]) for rows in pieces[1:]],
        sems,
    )
    later = fetch(
        [(gain_lat, hbuf), (wq_in, wq)]
        + [(latents.at[:, lax.rem(where[0] + k, NX)], lbuf.at[i]) for i, k in enumerate(FOREIGN)],
        sems.at[pl.ds(len(first), len(outs) + 2)],
    )
    back = fetch([(keys, keys_out), (values_t, values_out)], sems.at[pl.ds(0, 2)])
    for copy in first:
        copy.start()

    def ready(i):
        if i == 0:
            for copy in first[:4]:
                copy.wait()
            for copy in later:
                copy.start()
        else:
            first[3 + i].wait()

    project_points(pts, gbuf, wk, wv, keys, values_t, ybuf, ready)
    for copy in back:
        copy.start()
    later[0].wait()
    later[1].wait()
    row = gain_row(hbuf)
    for i, out in enumerate(outs):
        later[2 + i].wait()
        norm_rows(lbuf.at[i], row, xbuf)
        project_query(xbuf, wq, qbuf)
        attend_chunk(qbuf, keys, values_t, sbuf, pbuf, out)
    for copy in back:
        copy.wait()


def own_kernel(
    where, latents, gain, wq_in, keys_in, values_in, out,
    lbuf, gbuf, wq, keys, values_t, xbuf, qbuf, sbuf, pbuf, sems,
):
    copies = fetch(
        [(latents.at[:, where[0]], lbuf), (gain, gbuf), (wq_in, wq), (keys_in, keys), (values_in, values_t)],
        sems,
    )
    for copy in copies:
        copy.start()
    copies[0].wait()
    copies[1].wait()
    norm_rows(lbuf, gain_row(gbuf), xbuf)
    copies[2].wait()
    project_query(xbuf, wq, qbuf)
    copies[3].wait()
    copies[4].wait()
    attend_chunk(qbuf, keys, values_t, sbuf, pbuf, out)


def anywhere():
    return pl.BlockSpec(memory_space=pl.ANY)


def whole():
    return pl.BlockSpec(memory_space=pltpu.VMEM)


def anywhere():
    return pl.BlockSpec(memory_space=pl.ANY)


def attend_scratch(n):
    return [
        pltpu.VMEM((2, CHUNK, LANES), F32),
        pltpu.VMEM((2, n, LANES), BF16),
    ]


def encode_call(where, points, latents, gain_in, gain_lat, wk, wv, wq):
    n, width = points.shape
    nz, nx, rows, depth = latents.shape
    part = jax.ShapeDtypeStruct((nz * rows // LANES, 2, AUG, LANES), BF16)
    keys = jax.ShapeDtypeStruct((n, 2 * HS), BF16)
    values_t = jax.ShapeDtypeStruct((2, AUG, n), BF16)
    return pl.pallas_call(
        encode_kernel,
        out_shape=(part, part, part, keys, values_t),
        in_specs=[pl.BlockSpec(memory_space=pltpu.SMEM)] + [anywhere()] * 7,
        out_specs=(whole(), whole(), whole(), anywhere(), anywhere()),
        scratch_shapes=[
            pltpu.VMEM(points.shape, BF16),
            pltpu.VMEM((nx - 1, nz, rows, depth), BF16),
            pltpu.VMEM(gain_in.shape, F32),
            pltpu.VMEM(gain_lat.shape, F32),
            pltpu.VMEM(wk.shape, BF16),
            pltpu.VMEM(wv.shape, BF16),
            pltpu.VMEM(wq.shape, BF16),
            pltpu.VMEM(keys.shape, BF16),
            pltpu.VMEM(values_t.shape, BF16),
            pltpu.VMEM(points.shape, BF16),
            pltpu.VMEM((nz * rows, depth), BF16),
            pltpu.VMEM((nz * rows, 2 * HS), BF16),
        ]
        + attend_scratch(n)
        + [pltpu.SemaphoreType.DMA((n // PIECE + 8,))],
        compiler_params=pltpu.CompilerParams(vmem_limit_bytes=VMEM_WIDE),
        cost_estimate=pl.CostEstimate(
            flops=16 * 10**9, bytes_accessed=10**7, transcendentals=6 * 10**6
        ),
        name="encode",
    )(where, points, latents, gain_in, gain_lat, wk, wv, wq)


def own_call(where, latents, gain, wq, keys, values_t):
    nz, nx, rows, depth = latents.shape
    return pl.pallas_call(
        own_kernel,
        out_shape=jax.ShapeDtypeStruct((nz * rows // LANES, 2, AUG, LANES), BF16),
        in_specs=[pl.BlockSpec(memory_space=pltpu.SMEM)] + [anywhere()] * 5,
        out_specs=whole(),
        scratch_shapes=[
            pltpu.VMEM((nz, rows, depth), BF16),
            pltpu.VMEM(gain.shape, F32),
            pltpu.VMEM(wq.shape, BF16),
            pltpu.VMEM(keys.shape, BF16),
            pltpu.VMEM(values_t.shape, BF16),
            pltpu.VMEM((nz * rows, depth), BF16),
            pltpu.VMEM((nz * rows, 2 * HS), BF16),
        ]
        + attend_scratch(keys.shape[0])
        + [pltpu.SemaphoreType.DMA((5,))],
        compiler_params=pltpu.CompilerParams(vmem_limit_bytes=VMEM_WIDE),
        cost_estimate=pl.CostEstimate(
            flops=4 * 10**9, bytes_accessed=5 * 10**6, transcendentals=2 * 10**6
        ),
        name="own",
    )(where, latents, gain, wq, keys, values_t)


def merge(parts):
    shifts = [p[HS + 2 : HS + 3] + p[HS + 3 : HS + 4] for p in parts]
    high, low = split_pair(functools.reduce(jnp.maximum, shifts))
    top = high + low
    acc = functools.reduce(jnp.add, [p * jnp.exp2(s - top) for p, s in zip(parts, shifts)])
    return acc, acc[HS : HS + 1] + acc[HS + 1 : HS + 2], high, low


def combine_kernel(a, b, c, d, out):
    rows = out.shape[2] // 2
    per = LANES // rows
    for j in range(a.shape[0]):
        packed = []
        for h in range(2):
            acc, total, high, low = merge([r[j, h].astype(F32) for r in (a, b, c, d)])
            packed.append(with_stats(acc, total, high, low))
        for i in range(per):
            lanes = slice(i * rows, (i + 1) * rows)
            out[j * per + i] = jnp.concatenate([p[:, lanes] for p in packed], axis=1)


def finish(refs, rows):
    parts = [r[i].astype(F32) for r in refs for i in range(r.shape[0])]
    acc, total, _, _ = merge(parts)
    value = (acc[:HS] / total).T
    return jnp.concatenate([value[:rows], value[rows:]], axis=1).astype(BF16)


def finish_kernel(part, out):
    out[...] = finish([part], out.shape[0])


def near_kernel(a0, a1, a2, a3, w0, w1, w2, w3, out):
    total = None
    for a, w in ((a0, w0), (a1, w1), (a2, w2), (a3, w3)):
        term = jnp.dot(a[...], w[...], preferred_element_type=F32)
        total = term if total is None else total + term
    out[...] = total


def middle_kernel(latents, gain, own, other, wq, wk, wv, mid, q, kv):
    total = latents[...].astype(F32) + (own[...] + other[...])
    mid[...] = total
    x = normed(total, gain_row(gain))
    q[...] = lax.dot_general(x, wq[...], NT, preferred_element_type=F32).astype(BF16)
    k = lax.dot_general(x, wk[...], NT, preferred_element_type=F32).astype(BF16)
    v = lax.dot_general(x, wv[...], NT, preferred_element_type=F32).astype(BF16)
    both = jnp.concatenate([k, v], axis=1)
    for i in range(kv.shape[0]):
        kv[i] = both


def self_kernel(kv, q0, q1, q2, q3, out):
    scale = LOG2E * HS ** (-0.5)
    width = 2 * HS
    rows = q0.shape[0]
    keys = kv[:, 0:width]
    values_t = kv[:, width : 2 * width].astype(F32).T.astype(BF16)
    lane = lax.broadcasted_iota(jnp.int32, (rows, width), 1)
    first = lax.broadcasted_iota(jnp.int32, (HS, 2 * rows), 1) < rows
    for i, ref in enumerate((q0, q1, q2, q3)):
        q = ref[...]
        zero = jnp.zeros_like(q)
        both = jnp.concatenate([jnp.where(lane < HS, q, zero), jnp.where(lane < HS, zero, q)], axis=0)
        s = lax.dot_general(keys, both, NT, preferred_element_type=F32) * scale
        high, low = split_pair(jnp.max(s, axis=0, keepdims=True))
        p = jnp.exp2(s - (high + low))
        total = jnp.sum(p, axis=0, keepdims=True)
        n = jnp.dot(values_t, p.astype(BF16), preferred_element_type=F32)
        out[i] = with_stats(jnp.where(first, n[:HS], n[HS:]), total, high, low)


def output_kernel(p0, p1, p2, p3, w, out):
    count, rows, width = out.shape
    attn = finish([p0, p1, p2, p3], rows)
    terms = jnp.dot(attn, w[...], preferred_element_type=F32)
    for i in range(count):
        out[i] = terms[:, i * width : (i + 1) * width].astype(BF16)


def add_kernel(mid, terms, out):
    total = mid[...]
    for i in range(terms.shape[0]):
        total = total + terms[i].astype(F32)
    out[...] = total.astype(BF16)


def plain_call(kernel, name, out_shape, *args, flops=6 * 10**9):
    moved = sum(a.size * a.dtype.itemsize for a in args)
    spec = lambda a: pl.BlockSpec(memory_space=pltpu.SMEM) if a.dtype == jnp.int32 else whole()
    return pl.pallas_call(
        kernel,
        out_shape=out_shape,
        in_specs=[spec(a) for a in args],
        out_specs=jax.tree.map(lambda _: whole(), out_shape),
        compiler_params=pltpu.CompilerParams(vmem_limit_bytes=VMEM_LIMIT),
        cost_estimate=pl.CostEstimate(flops=flops, bytes_accessed=moved, transcendentals=0),
        name=name,
    )(*args)


def permute_x(v, k):
    return lax.ppermute(
        v, "seq", [(i, (i // NX) * NX + (i % NX + k) % NX) for i in range(NX * NZ)]
    )


def permute_y(v, k):
    return lax.ppermute(v, "head", [(i, (i + 2 * k) % (2 * NY)) for i in range(2 * NY)])


def swap_cores(v):
    return lax.ppermute(v, "head", [(i, i ^ 1) for i in range(2 * NY)])


def gather_y(v):
    return [v] + [permute_y(v, k) for k in FOREIGN]


def body(
    points,
    latents,
    gain_in,
    gain_lat,
    gain_self,
    cross_query,
    cross_key,
    cross_value,
    cross_out,
    self_query,
    latent_key_weight,
    self_value,
    self_out,
):
    width = cross_query.shape[1]
    count, depth = latents.shape
    rows = count // (NX * NZ)
    seq = lax.axis_index("seq").astype(jnp.int32)
    head = lax.axis_index("head").astype(jnp.int32)
    part_shape = jax.ShapeDtypeStruct((NZ, AUG, 2 * rows), BF16)
    gains = [g.reshape(-1, 128) for g in (gain_in, gain_lat, gain_self)]

    out_near = [cross_out] + [permute_y(cross_out, k) for k in FOREIGN[1:]]
    latents_4d = latents.reshape(NZ, NX, rows, depth)
    x = (seq % NX).reshape(1)
    *sent, keys, values_t = encode_call(
        x, points, latents_4d, gains[0], gains[1], cross_key.T, cross_value.T, cross_query.T
    )
    parts = [permute_x(v, k) for v, k in zip(sent, FOREIGN)]
    part = own_call(x, latents_4d, gains[1], cross_query.T, keys, values_t)
    part = plain_call(combine_kernel, "combine", part_shape, part, *parts)
    part, last = lax.optimization_barrier((part, cross_out))
    out_near.insert(1, permute_y(last, FOREIGN[0]))
    lat_rows = lax.dynamic_slice_in_dim(latents, seq * rows, rows, 0)
    part = lax.all_to_all(part, "seq", 0, 0, axis_index_groups=Z_GROUPS)
    part, out_near, lat_rows = lax.optimization_barrier((part, out_near, lat_rows))
    block = jax.ShapeDtypeStruct((rows, width), BF16)
    cross_attn = plain_call(finish_kernel, "finish", block, part)
    own = plain_call(
        near_kernel, "near", jax.ShapeDtypeStruct((rows, depth), F32), *gather_y(cross_attn), *out_near
    )
    mid, squery, kv = plain_call(
        middle_kernel, "middle",
        (
            jax.ShapeDtypeStruct((rows, depth), F32),
            block,
            jax.ShapeDtypeStruct((NZ, rows, 2 * width), BF16),
        ),
        lat_rows, gains[2], own, swap_cores(own),
        self_query.T, latent_key_weight.T, self_value.T,
    )
    kv = lax.all_to_all(kv, "seq", 0, 0, axis_index_groups=Z_GROUPS)
    squeries = [squery] + [permute_x(squery, k) for k in SHIFTS]
    mid_cols = lax.dynamic_slice_in_dim(mid, head * width, width, 1)
    kv, mid_cols = lax.optimization_barrier((kv, mid_cols))
    part = plain_call(
        self_kernel, "self_part", jax.ShapeDtypeStruct((NX, AUG, 2 * rows), BF16),
        kv.reshape(NZ * rows, 2 * width), *squeries,
    )
    back = [part[0:1]] + [permute_x(part[i + 1 : i + 2], -k) for i, k in enumerate(SHIFTS)]
    terms = plain_call(
        output_kernel, "output", jax.ShapeDtypeStruct((2 * NY, rows, width), BF16), *back, self_out
    )
    terms = lax.all_to_all(terms, "head", 0, 0)
    return plain_call(add_kernel, "add", block, mid_cols, terms)


def solution(mesh):
    in_specs = (
        P("seq", None),
        P(),
        P(),
        P(),
        P(),
        P(None, "head"),
        P(None, "head"),
        P(None, "head"),
        P("head", None),
        P(None, "head"),
        P(None, "head"),
        P(None, "head"),
        P("head", None),
    )
    out_specs = P("seq", "head")
    return jax.shard_map(body, mesh=mesh, in_specs=in_specs, out_specs=out_specs, check_vma=False)
```

```python
import functools
import jax
import jax.numpy as jnp
from jax import lax
from jax.experimental import pallas as pl
from jax.experimental.pallas import tpu as pltpu
from jax.sharding import PartitionSpec as P

NX = 4
NY = 4
NZ = 8
Z_GROUPS = [[z * NX + x for z in range(NZ)] for x in range(NX)]
SHIFTS = (1, NX - 1, 2)
FOREIGN = (2, 1, NX - 1)

HS = 96
AUG = 112
LANES = 256
CHUNK = 256
PIECE = 512
LOG2E = 1.4426950408889634
SAFE = 2.0**64
F32 = jnp.float32
BF16 = jnp.bfloat16
NT = (((1,), (1,)), ((), ()))
VMEM_LIMIT = 20 * 1024 * 1024
VMEM_WIDE = 58 * 1024 * 1024


def normed(values, gain):
    values = values.astype(F32)
    center = values - jnp.mean(values, axis=-1, keepdims=True)
    spread = jnp.mean(center * center, axis=-1, keepdims=True)
    return (center * lax.rsqrt(spread + 1e-05) * gain).astype(BF16)


def gain_row(gain):
    return jnp.concatenate([gain[i : i + 1, :] for i in range(gain.shape[0])], axis=1)


def split_pair(value):
    high = value.astype(BF16).astype(F32)
    return high, (value - high).astype(BF16).astype(F32)


def fetch(pairs, sems):
    return [pltpu.make_async_copy(src, dst, sems.at[i]) for i, (src, dst) in enumerate(pairs)]


def project_points(pbuf, gain, wk, wv, keys, values_t, xbuf, ready):
    for i in range(pbuf.shape[0] // PIECE):
        ready(i)
        row = gain_row(gain)
        for j in range(i * PIECE, (i + 1) * PIECE, 64):
            xbuf[j : j + 64, :] = normed(pbuf[j : j + 64, :], row)
    x = xbuf[...]
    keys[...] = lax.dot_general(x, wk[...], NT, preferred_element_type=F32).astype(BF16)
    vt = lax.dot_general(wv[...], x, NT, preferred_element_type=F32).astype(BF16)
    for h in range(2):
        values_t[h, 0:HS, :] = vt[h * HS : (h + 1) * HS]
    one = lax.broadcasted_iota(jnp.int32, (AUG - HS, pbuf.shape[0]), 0) == 0
    for h in range(2):
        values_t[h, HS:AUG, :] = one.astype(BF16)


def attend_units(queries, keys, values_t, sbuf, pbuf, emit):
    count = keys.shape[0]
    scale = LOG2E * HS ** (-0.5)
    chunks = count // CHUNK

    def score(u, c):
        rows = pl.ds(c * CHUNK, CHUNK)
        return lax.dot_general(keys[rows, :], queries[u][1], NT, preferred_element_type=F32)

    def first(u):
        s = score(u, 0)
        sbuf[u % 2] = s
        return split_pair(jnp.max(s, axis=0, keepdims=True) * scale)

    largest = jnp.zeros((1, LANES), F32)
    state = first(0)
    for u, (h, q) in enumerate(queries):
        high, low = state
        shift = high + low
        for c in range(chunks):
            s = sbuf[u % 2] if c == 0 else score(u, c)
            pbuf[u % 2, c * CHUNK : (c + 1) * CHUNK, :] = jnp.exp2(s * scale - shift).astype(BF16)
        acc = jnp.dot(values_t[h], pbuf[u % 2], preferred_element_type=F32)
        if u + 1 < len(queries):
            state = first(u + 1)
        emit(u, acc, high, low)
        largest = jnp.maximum(largest, acc[HS : HS + 1])
    return jnp.max(largest)


def attend_exact(h, q, keys, values_t):
    scale = LOG2E * HS ** (-0.5)
    chunks = keys.shape[0] // CHUNK

    def scores(c):
        rows = pl.ds(pl.multiple_of(c * CHUNK, CHUNK), CHUNK)
        s = lax.dot_general(keys[rows, :], q, NT, preferred_element_type=F32)
        return s * scale

    def largest(c, top):
        return jnp.maximum(top, jnp.max(scores(c), axis=0, keepdims=True))

    top = lax.fori_loop(0, chunks, largest, jnp.full((1, LANES), -jnp.inf, F32))
    high, low = split_pair(top)
    shift = high + low

    def add(c, acc):
        rows = pl.ds(pl.multiple_of(c * CHUNK, CHUNK), CHUNK)
        p = jnp.exp2(scores(c) - shift).astype(BF16)
        return acc + jnp.dot(values_t[h, :, rows], p, preferred_element_type=F32)

    acc = lax.fori_loop(0, chunks, add, jnp.zeros((AUG, LANES), F32))
    return acc, high, low


def with_stats(acc, total, high, low):
    total_high, total_low = split_pair(total)
    row = lax.broadcasted_iota(jnp.int32, (AUG - HS, acc.shape[1]), 0)
    stats = jnp.where(row == 0, total_high, 0.0)
    stats = jnp.where(row == 1, total_low, stats)
    stats = jnp.where(row == 2, high, stats)
    stats = jnp.where(row == 3, low, stats)
    return jnp.concatenate([acc[:HS], stats], axis=0).astype(BF16)


def attend_chunk(qbuf, keys, values_t, sbuf, pbuf, out):
    blocks = qbuf.shape[0] // LANES

    def query(j, h):
        start = j * LANES if isinstance(j, int) else pl.multiple_of(j * LANES, LANES)
        q = qbuf[pl.ds(start, LANES), :]
        lane = lax.broadcasted_iota(jnp.int32, q.shape, 1)
        return jnp.where((lane < HS) == (h == 0), q, jnp.zeros_like(q))

    def emit_at(j, h, acc, high, low):
        out[j, h] = with_stats(acc, acc[HS : HS + 1], high, low)

    queries = [(h, query(j, h)) for j in range(blocks) for h in range(2)]
    above = attend_units(
        queries, keys, values_t, sbuf, pbuf, lambda u, *r: emit_at(u // 2, u % 2, *r)
    )

    @pl.when(jnp.logical_not(above <= SAFE))
    def _():
        def again(j, carry):
            for h in range(2):
                emit_at(j, h, *attend_exact(h, query(j, h), keys, values_t))
            return carry

        lax.fori_loop(0, blocks, again, 0)


def norm_rows(lbuf, row, xbuf, ready=lambda z: None):
    rows, width = lbuf.shape[1], lbuf.shape[2]
    for z in range(lbuf.shape[0]):
        ready(z)
        part = pl.ds(z * rows, rows)
        x = lbuf[z].astype(F32)
        off = x - x[:, 0:1]
        mean = jnp.sum(off, axis=-1, keepdims=True) * (1.0 / width)
        spread = jnp.sum(off * off, axis=-1, keepdims=True) * (1.0 / width) - mean * mean
        factor = lax.rsqrt(jnp.maximum(spread, 0.0) + 1e-05)
        xbuf[part, :] = ((off - mean) * factor * row).astype(BF16)


def project_query(xbuf, wq, qbuf):
    qbuf[...] = lax.dot_general(xbuf[...], wq[...], NT, preferred_element_type=F32).astype(BF16)


def encode_kernel(
    where, points, latents, gain_in, gain_lat, wk_in, wv_in, wq_in,
    out0, out1, out2, keys_out, values_out,
    pts, lbuf, gbuf, hbuf, wk, wv, wq, keys, values_t, ybuf, xbuf, qbuf, sbuf, pbuf, sems,
):
    outs = (out0, out1, out2)
    pieces = [pl.ds(i * PIECE, PIECE) for i in range(pts.shape[0] // PIECE)]
    first = fetch(
        [(points.at[pieces[0], :], pts.at[pieces[0], :]), (gain_in, gbuf), (wk_in, wk), (wv_in, wv)]
        + [(points.at[rows, :], pts.at[rows, :]) for rows in pieces[1:]],
        sems,
    )
    later = fetch(
        [(gain_lat, hbuf), (wq_in, wq)]
        + [(latents.at[:, lax.rem(where[0] + k, NX)], lbuf.at[i]) for i, k in enumerate(FOREIGN)],
        sems.at[pl.ds(len(first), len(outs) + 2)],
    )
    back = fetch([(keys, keys_out), (values_t, values_out)], sems.at[pl.ds(0, 2)])
    for copy in first:
        copy.start()

    def ready(i):
        if i == 0:
            for copy in first[:4]:
                copy.wait()
            for copy in later:
                copy.start()
        else:
            first[3 + i].wait()

    project_points(pts, gbuf, wk, wv, keys, values_t, ybuf, ready)
    for copy in back:
        copy.start()
    later[0].wait()
    later[1].wait()
    row = gain_row(hbuf)
    for i, out in enumerate(outs):
        later[2 + i].wait()
        norm_rows(lbuf.at[i], row, xbuf)
        project_query(xbuf, wq, qbuf)
        attend_chunk(qbuf, keys, values_t, sbuf, pbuf, out)
    for copy in back:
        copy.wait()


def own_kernel(
    where, latents, gain, wq_in, keys_in, values_in, out,
    lbuf, gbuf, wq, keys, values_t, xbuf, qbuf, sbuf, pbuf, sems,
):
    nz = lbuf.shape[0]
    copies = fetch(
        [(gain, gbuf)]
        + [(latents.at[z, where[0]], lbuf.at[z]) for z in range(nz)]
        + [(wq_in, wq), (keys_in, keys), (values_in, values_t)],
        sems,
    )
    for copy in copies:
        copy.start()
    copies[0].wait()
    norm_rows(lbuf, gain_row(gbuf), xbuf, lambda z: copies[1 + z].wait())
    copies[1 + nz].wait()
    project_query(xbuf, wq, qbuf)
    copies[2 + nz].wait()
    copies[3 + nz].wait()
    attend_chunk(qbuf, keys, values_t, sbuf, pbuf, out)


def anywhere():
    return pl.BlockSpec(memory_space=pl.ANY)


def whole():
    return pl.BlockSpec(memory_space=pltpu.VMEM)


def anywhere():
    return pl.BlockSpec(memory_space=pl.ANY)


def attend_scratch(n):
    return [
        pltpu.VMEM((2, CHUNK, LANES), F32),
        pltpu.VMEM((2, n, LANES), BF16),
    ]


def encode_call(where, points, latents, gain_in, gain_lat, wk, wv, wq):
    n, width = points.shape
    nz, nx, rows, depth = latents.shape
    part = jax.ShapeDtypeStruct((nz * rows // LANES, 2, AUG, LANES), BF16)
    keys = jax.ShapeDtypeStruct((n, 2 * HS), BF16)
    values_t = jax.ShapeDtypeStruct((2, AUG, n), BF16)
    return pl.pallas_call(
        encode_kernel,
        out_shape=(part, part, part, keys, values_t),
        in_specs=[pl.BlockSpec(memory_space=pltpu.SMEM)] + [anywhere()] * 7,
        out_specs=(whole(), whole(), whole(), anywhere(), anywhere()),
        scratch_shapes=[
            pltpu.VMEM(points.shape, BF16),
            pltpu.VMEM((nx - 1, nz, rows, depth), BF16),
            pltpu.VMEM(gain_in.shape, F32),
            pltpu.VMEM(gain_lat.shape, F32),
            pltpu.VMEM(wk.shape, BF16),
            pltpu.VMEM(wv.shape, BF16),
            pltpu.VMEM(wq.shape, BF16),
            pltpu.VMEM(keys.shape, BF16),
            pltpu.VMEM(values_t.shape, BF16),
            pltpu.VMEM(points.shape, BF16),
            pltpu.VMEM((nz * rows, depth), BF16),
            pltpu.VMEM((nz * rows, 2 * HS), BF16),
        ]
        + attend_scratch(n)
        + [pltpu.SemaphoreType.DMA((n // PIECE + 8,))],
        compiler_params=pltpu.CompilerParams(vmem_limit_bytes=VMEM_WIDE),
        cost_estimate=pl.CostEstimate(
            flops=16 * 10**9, bytes_accessed=10**7, transcendentals=6 * 10**6
        ),
        name="encode",
    )(where, points, latents, gain_in, gain_lat, wk, wv, wq)


def own_call(where, latents, gain, wq, keys, values_t):
    nz, nx, rows, depth = latents.shape
    return pl.pallas_call(
        own_kernel,
        out_shape=jax.ShapeDtypeStruct((nz * rows // LANES, 2, AUG, LANES), BF16),
        in_specs=[pl.BlockSpec(memory_space=pltpu.SMEM)] + [anywhere()] * 5,
        out_specs=whole(),
        scratch_shapes=[
            pltpu.VMEM((nz, rows, depth), BF16),
            pltpu.VMEM(gain.shape, F32),
            pltpu.VMEM(wq.shape, BF16),
            pltpu.VMEM(keys.shape, BF16),
            pltpu.VMEM(values_t.shape, BF16),
            pltpu.VMEM((nz * rows, depth), BF16),
            pltpu.VMEM((nz * rows, 2 * HS), BF16),
        ]
        + attend_scratch(keys.shape[0])
        + [pltpu.SemaphoreType.DMA((nz + 4,))],
        compiler_params=pltpu.CompilerParams(vmem_limit_bytes=VMEM_WIDE),
        cost_estimate=pl.CostEstimate(
            flops=4 * 10**9, bytes_accessed=5 * 10**6, transcendentals=2 * 10**6
        ),
        name="own",
    )(where, latents, gain, wq, keys, values_t)


def merge(parts):
    shifts = [p[HS + 2 : HS + 3] + p[HS + 3 : HS + 4] for p in parts]
    high, low = split_pair(functools.reduce(jnp.maximum, shifts))
    top = high + low
    acc = functools.reduce(jnp.add, [p * jnp.exp2(s - top) for p, s in zip(parts, shifts)])
    return acc, acc[HS : HS + 1] + acc[HS + 1 : HS + 2], high, low


def combine_kernel(a, b, c, d, out):
    rows = out.shape[2] // 2
    per = LANES // rows
    for j in range(a.shape[0]):
        packed = []
        for h in range(2):
            acc, total, high, low = merge([r[j, h].astype(F32) for r in (a, b, c, d)])
            packed.append(with_stats(acc, total, high, low))
        for i in range(per):
            lanes = slice(i * rows, (i + 1) * rows)
            out[j * per + i] = jnp.concatenate([p[:, lanes] for p in packed], axis=1)


def finish(refs, rows):
    parts = [r[i].astype(F32) for r in refs for i in range(r.shape[0])]
    acc, total, _, _ = merge(parts)
    value = (acc[:HS] / total).T
    return jnp.concatenate([value[:rows], value[rows:]], axis=1).astype(BF16)


def finish_kernel(part, out):
    out[...] = finish([part], out.shape[0])


def near_kernel(a0, a1, a2, a3, w0, w1, w2, w3, out):
    total = None
    for a, w in ((a0, w0), (a1, w1), (a2, w2), (a3, w3)):
        term = jnp.dot(a[...], w[...], preferred_element_type=F32)
        total = term if total is None else total + term
    out[...] = total


def middle_kernel(latents, gain, own, other, wq, wk, wv, mid, q, kv):
    total = latents[...].astype(F32) + (own[...] + other[...])
    mid[...] = total
    x = normed(total, gain_row(gain))
    q[...] = lax.dot_general(x, wq[...], NT, preferred_element_type=F32).astype(BF16)
    k = lax.dot_general(x, wk[...], NT, preferred_element_type=F32).astype(BF16)
    v = lax.dot_general(x, wv[...], NT, preferred_element_type=F32).astype(BF16)
    both = jnp.concatenate([k, v], axis=1)
    for i in range(kv.shape[0]):
        kv[i] = both


def self_kernel(kv, q0, q1, q2, q3, out):
    scale = LOG2E * HS ** (-0.5)
    width = 2 * HS
    rows = q0.shape[0]
    keys = kv[:, 0:width]
    values_t = kv[:, width : 2 * width].astype(F32).T.astype(BF16)
    lane = lax.broadcasted_iota(jnp.int32, (rows, width), 1)
    first = lax.broadcasted_iota(jnp.int32, (HS, 2 * rows), 1) < rows
    for i, ref in enumerate((q0, q1, q2, q3)):
        q = ref[...]
        zero = jnp.zeros_like(q)
        both = jnp.concatenate([jnp.where(lane < HS, q, zero), jnp.where(lane < HS, zero, q)], axis=0)
        s = lax.dot_general(keys, both, NT, preferred_element_type=F32) * scale
        high, low = split_pair(jnp.max(s, axis=0, keepdims=True))
        p = jnp.exp2(s - (high + low))
        total = jnp.sum(p, axis=0, keepdims=True)
        n = jnp.dot(values_t, p.astype(BF16), preferred_element_type=F32)
        out[i] = with_stats(jnp.where(first, n[:HS], n[HS:]), total, high, low)


def output_kernel(p0, p1, p2, p3, w, out):
    count, rows, width = out.shape
    attn = finish([p0, p1, p2, p3], rows)
    terms = jnp.dot(attn, w[...], preferred_element_type=F32)
    for i in range(count):
        out[i] = terms[:, i * width : (i + 1) * width].astype(BF16)


def add_kernel(mid, terms, out):
    total = mid[...]
    for i in range(terms.shape[0]):
        total = total + terms[i].astype(F32)
    out[...] = total.astype(BF16)


def plain_call(kernel, name, out_shape, *args, flops=6 * 10**9):
    moved = sum(a.size * a.dtype.itemsize for a in args)
    spec = lambda a: pl.BlockSpec(memory_space=pltpu.SMEM) if a.dtype == jnp.int32 else whole()
    return pl.pallas_call(
        kernel,
        out_shape=out_shape,
        in_specs=[spec(a) for a in args],
        out_specs=jax.tree.map(lambda _: whole(), out_shape),
        compiler_params=pltpu.CompilerParams(vmem_limit_bytes=VMEM_LIMIT),
        cost_estimate=pl.CostEstimate(flops=flops, bytes_accessed=moved, transcendentals=0),
        name=name,
    )(*args)


def permute_x(v, k):
    return lax.ppermute(
        v, "seq", [(i, (i // NX) * NX + (i % NX + k) % NX) for i in range(NX * NZ)]
    )


def permute_y(v, k):
    return lax.ppermute(v, "head", [(i, (i + 2 * k) % (2 * NY)) for i in range(2 * NY)])


def swap_cores(v):
    return lax.ppermute(v, "head", [(i, i ^ 1) for i in range(2 * NY)])


def gather_y(v):
    got = {k: permute_y(v, k) for k in FOREIGN}
    return [v] + [got[k] for k in SHIFTS]


def body(
    points,
    latents,
    gain_in,
    gain_lat,
    gain_self,
    cross_query,
    cross_key,
    cross_value,
    cross_out,
    self_query,
    latent_key_weight,
    self_value,
    self_out,
):
    width = cross_query.shape[1]
    count, depth = latents.shape
    rows = count // (NX * NZ)
    seq = lax.axis_index("seq").astype(jnp.int32)
    head = lax.axis_index("head").astype(jnp.int32)
    part_shape = jax.ShapeDtypeStruct((NZ, AUG, 2 * rows), BF16)
    gains = [g.reshape(-1, 128) for g in (gain_in, gain_lat, gain_self)]

    out_near = [cross_out] + [permute_y(cross_out, k) for k in SHIFTS[:2]]
    latents_4d = latents.reshape(NZ, NX, rows, depth)
    x = (seq % NX).reshape(1)
    *sent, keys, values_t = encode_call(
        x, points, latents_4d, gains[0], gains[1], cross_key.T, cross_value.T, cross_query.T
    )
    parts = [permute_x(v, k) for v, k in zip(sent, FOREIGN)]
    part = own_call(x, latents_4d, gains[1], cross_query.T, keys, values_t)
    part = plain_call(combine_kernel, "combine", part_shape, part, *parts)
    part, last = lax.optimization_barrier((part, cross_out))
    out_near.append(permute_y(last, SHIFTS[2]))
    lat_rows = lax.dynamic_slice_in_dim(latents, seq * rows, rows, 0)
    part = lax.all_to_all(part, "seq", 0, 0, axis_index_groups=Z_GROUPS)
    part, out_near, lat_rows = lax.optimization_barrier((part, out_near, lat_rows))
    block = jax.ShapeDtypeStruct((rows, width), BF16)
    cross_attn = plain_call(finish_kernel, "finish", block, part)
    own = plain_call(
        near_kernel, "near", jax.ShapeDtypeStruct((rows, depth), F32), *gather_y(cross_attn), *out_near
    )
    mid, squery, kv = plain_call(
        middle_kernel, "middle",
        (
            jax.ShapeDtypeStruct((rows, depth), F32),
            block,
            jax.ShapeDtypeStruct((NZ, rows, 2 * width), BF16),
        ),
        lat_rows, gains[2], own, swap_cores(own),
        self_query.T, latent_key_weight.T, self_value.T,
    )
    kv = lax.all_to_all(kv, "seq", 0, 0, axis_index_groups=Z_GROUPS)
    squeries = [squery] + [permute_x(squery, k) for k in SHIFTS]
    mid_cols = lax.dynamic_slice_in_dim(mid, head * width, width, 1)
    kv, mid_cols = lax.optimization_barrier((kv, mid_cols))
    part = plain_call(
        self_kernel, "self_part", jax.ShapeDtypeStruct((NX, AUG, 2 * rows), BF16),
        kv.reshape(NZ * rows, 2 * width), *squeries,
    )
    back = [part[0:1]] + [permute_x(part[i + 1 : i + 2], -k) for i, k in enumerate(SHIFTS)]
    terms = plain_call(
        output_kernel, "output", jax.ShapeDtypeStruct((2 * NY, rows, width), BF16), *back, self_out
    )
    terms = lax.all_to_all(terms, "head", 0, 0)
    return plain_call(add_kernel, "add", block, mid_cols, terms)


def solution(mesh):
    in_specs = (
        P("seq", None),
        P(),
        P(),
        P(),
        P(),
        P(None, "head"),
        P(None, "head"),
        P(None, "head"),
        P("head", None),
        P(None, "head"),
        P(None, "head"),
        P(None, "head"),
        P("head", None),
    )
    out_specs = P("seq", "head")
    return jax.shard_map(body, mesh=mesh, in_specs=in_specs, out_specs=out_specs, check_vma=False)
```
